32 devices in a mesh: parts: 2 (over x), expert: 16 (over z, y, core).
Axes of the slice: x: 2, y: 2, z: 4, core: 2. Of those that a mesh axis runs over, the one named last changes fastest.
Arguments:
- tokens: bfloat16 [4096, 2048], P(('parts', 'expert')), parts along dimension 0, may hold values from -6 to 6
- cotangent: bfloat16 [4096, 2048], P(('parts', 'expert')), parts along dimension 0, may hold values from -1.25 to 1.25
- expert_ids: int32 [4096, 4], P(('parts', 'expert')), parts along dimension 0, may hold values from 0 to 15, as said below
- gate_weights: bfloat16 [4096, 4], P(('parts', 'expert')), parts along dimension 0, may hold values from 0.099609375 to 1
- w_gate_up: bfloat16 [32, 2048, 1536], P(('parts', 'expert')), parts along dimension 0, may hold values from -0.125 to 0.125
- w_down: bfloat16 [32, 768, 2048], P(('parts', 'expert')), parts along dimension 0, may hold values from -0.21875 to 0.21875
Outputs:
- grad_tokens: bfloat16 [4096, 2048], P(('parts', 'expert')), parts along dimension 0
- grad_gates: bfloat16 [4096, 4], P(('parts', 'expert')), parts along dimension 0
The draws below stay inside these ranges and needn't reach their ends.
There are 2 independent parts, one for each index of `parts`. The reference program is written for one: setup_inputs(seed, part) draws one part's arguments, and reference() takes and returns one part's arrays. A program takes and returns all parts, laid end to end along the dimension named above; each array names one. Nothing has to cross between parts.
Inputs may be any that keep to these rules, and one draw needn't show every extreme that they name: `expert_ids`: each token names 4 different experts. Among the tokens of one device no expert is named more than 56 times, and one expert is named exactly 56 times by the tokens of every device.
All inputs are finite; a program needn't handle non-finite values.
Results may differ from the reference program's by a relative error of at most 0.0058.
Values may be sent and summed in bfloat16 or wider, within the bound.
No kernel may reach another device: no remote copies, remote signals or barrier semaphores. Data moves between devices by JAX's collectives and lax.ppermute only.
A program may use at most 128 MiB of HBM per device.

```python
import jax
import jax.numpy as jnp
from jax import lax

D = 2048
FF = 768
TOP = 4
TOK_DEV = 128
EXPERTS = 16
TOKENS = 2048
CAP = 56
SLOTS = 896
N_EXPERT = 16


def draw_expert_ids(key, part):
    key = jax.random.fold_in(key, 7)
    hottest = jax.random.randint(jax.random.fold_in(key, 1), (), 0, EXPERTS)
    spread_count = TOK_DEV * TOP - CAP

    def one_block(block_key):
        first_key, second_key, third_key = jax.random.split(block_key, 3)
        shuffled = jax.random.permutation(first_key, (EXPERTS - 1) * CAP)
        chosen = jnp.sort(shuffled[:spread_count])
        others = (chosen // CAP).astype(jnp.int32)
        others = others + (others >= hottest).astype(jnp.int32)
        listing = jnp.concatenate([jnp.full((CAP,), hottest, jnp.int32), others])
        table = listing.reshape(TOP, TOK_DEV).T
        table = table[jax.random.permutation(second_key, TOK_DEV)]
        scores = jax.random.randint(third_key, (TOK_DEV, TOP), 0, 1 << 20) * TOP + jnp.arange(TOP, dtype=jnp.int32)[None, :]
        ordering = jnp.argsort(scores, axis=1)
        return jnp.take_along_axis(table, ordering, axis=1)
    block_keys = jax.random.split(jax.random.fold_in(key, 2), N_EXPERT)
    return jax.vmap(one_block)(block_keys).reshape(N_EXPERT * TOK_DEV, TOP).astype(jnp.int32)


def shard_levels(rng, extent, shards, smallest, largest):
    gain, own = 1.0, jax.random.fold_in(rng, 6)
    for position, blocks in shards:
        steps = jnp.exp(jax.random.uniform(jax.random.fold_in(own, position), (blocks,), jnp.float32, smallest / len(shards), largest / len(shards)))
        gain = gain * jnp.repeat(steps, extent[position] // blocks).reshape([-1 if axis == position else 1 for axis in range(len(extent))])
    return gain


def scatter_about(rng, extent, deviation, bound, pieces=(), held_as=jnp.bfloat16):
    values = deviation * jax.random.normal(rng, extent, jnp.float32)
    if pieces:
        values = values * shard_levels(rng, extent, pieces, -0.22, 0.18)
    return jnp.clip(values, -bound, bound).astype(held_as)


def setup_inputs(seed: int = 0, part: int = 0) -> dict:
    key_of = jax.random.split(jax.random.key(seed), 7)
    part_keys = jax.random.split(jax.random.fold_in(key_of[6], part), 7)
    tokens = scatter_about(part_keys[0], (TOKENS, D), 1.0, 6.0, ((0, 16),))
    cotangent = scatter_about(part_keys[1], (TOKENS, D), 0.2, 1.25, ((0, 16),))
    expert_ids = draw_expert_ids(jax.random.fold_in(jax.random.fold_in(key_of[6], part), 71), part)
    gate_weights = jnp.clip(0.099609375 + 0.9003906 * jax.random.uniform(part_keys[3], (TOKENS, TOP), jnp.float32) ** shard_levels(part_keys[3], (TOKENS, TOP), ((0, 16),), -0.2, 0.2), 0.099609375, 1.0).astype(jnp.bfloat16)
    w_gate_up = scatter_about(part_keys[4], (EXPERTS, D, 2 * FF), D ** -0.5, 0.125, ((0, 16),))
    w_down = scatter_about(part_keys[5], (EXPERTS, FF, D), FF ** -0.5, 0.21875, ((0, 16),))
    return {"tokens": tokens, "cotangent": cotangent, "expert_ids": expert_ids, "gate_weights": gate_weights, "w_gate_up": w_gate_up, "w_down": w_down}


def finish(projections, grads_in, weights_in, joined, down_matrix):
    gate_pre = projections[:, :FF]
    up_pre = projections[:, FF:]
    sigmoid_gate = jax.nn.sigmoid(gate_pre)
    active = gate_pre * sigmoid_gate
    hidden = active * up_pre
    hidden_grad = lax.dot_general(grads_in, down_matrix, (((1,), (1,)), ((), ())), preferred_element_type=jnp.float32)
    gate_grad = jnp.sum(hidden_grad * hidden, axis=1).astype(jnp.bfloat16)
    scaled = weights_in.astype(jnp.float32)[:, None] * hidden_grad
    first_half = scaled * up_pre * sigmoid_gate * (1.0 + gate_pre * (1.0 - sigmoid_gate))
    second_half = scaled * active
    projection_grad = jnp.concatenate([first_half, second_half], axis=1).astype(jnp.bfloat16)
    route_grad = lax.dot_general(projection_grad, joined, (((1,), (1,)), ((), ())), preferred_element_type=jnp.float32)
    return route_grad.astype(jnp.bfloat16), gate_grad


def reference(tokens, cotangent, expert_ids, gate_weights, w_gate_up, w_down):
    route_total = TOKENS * TOP
    flat_ids = expert_ids.reshape(route_total).astype(jnp.int32)
    onehot = (flat_ids[:, None] == jnp.arange(EXPERTS, dtype=jnp.int32)[None, :]).astype(jnp.int32)
    blocked = onehot.reshape(N_EXPERT, TOK_DEV * TOP, EXPERTS)
    rank_in = jnp.sum((jnp.cumsum(blocked, axis=1) - blocked) * blocked, axis=2).reshape(route_total)
    source_dev = jnp.arange(route_total, dtype=jnp.int32) // (TOK_DEV * TOP)
    target = flat_ids * SLOTS + source_dev * CAP + rank_in
    filler = jnp.zeros((EXPERTS * SLOTS,), jnp.int32).at[target].set(jnp.arange(1, route_total + 1, dtype=jnp.int32))
    filler = filler.reshape(EXPERTS, SLOTS)
    flat_gates = gate_weights.reshape(route_total)

    def expert_step(carry, inputs):
        token_acc, gate_acc = carry
        filler_row, joined, down_matrix = inputs
        in_use = filler_row > 0
        route_id = jnp.maximum(filler_row - 1, 0).astype(jnp.int32)
        token_id = (route_id // TOP).astype(jnp.int32)
        rows_in = jnp.where(in_use[:, None], tokens[token_id], 0)
        grads_in = jnp.where(in_use[:, None], cotangent[token_id], 0)
        weights_in = jnp.where(in_use, flat_gates[route_id], 0)
        projections = jnp.dot(rows_in, joined, preferred_element_type=jnp.float32)
        route_grad, gate_grad = finish(projections, grads_in, weights_in, joined, down_matrix)
        token_acc = token_acc.at[token_id].add(jnp.where(in_use[:, None], route_grad.astype(jnp.float32), jnp.float32(0.0)))
        gate_acc = gate_acc.at[route_id].add(jnp.where(in_use, gate_grad.astype(jnp.float32), jnp.float32(0.0)))
        return (token_acc, gate_acc), jnp.float32(0.0)

    start_state = (jnp.zeros((TOKENS, D), jnp.float32), jnp.zeros((route_total,), jnp.float32))
    result = lax.scan(expert_step, start_state, (filler, w_gate_up, w_down))
    token_acc, gate_acc = result[0]
    return token_acc.astype(jnp.bfloat16), gate_acc.reshape(TOKENS, TOP).astype(jnp.bfloat16)
```

```python
import functools

import jax
import jax.numpy as jnp
from jax import lax
from jax.experimental import pallas as pl
from jax.experimental.pallas import tpu as pltpu
from jax.sharding import PartitionSpec as P

F32, BF16 = jnp.float32, jnp.bfloat16
LANES = 128
VMEM_BYTES = 48 * 2**20
NT = (((1,), (1,)), ((), ()))


def project_kernel(rows, features, own_ref, far_ref, w0_ref, w1_ref, out0_ref, out1_ref, both):
    @pl.when(pl.program_id(0) == 0)
    def _():
        both[:rows, :] = own_ref[:, :features]
        both[rows:, :] = far_ref[:, :features]

    out0_ref[...] = jnp.dot(both[...], w0_ref[...], preferred_element_type=F32)
    out1_ref[...] = jnp.dot(both[...], w1_ref[...], preferred_element_type=F32)


def project(own, far, w0, w1, tile=384):
    rows = own.shape[0]
    features, width = w0.shape
    whole = lambda a: pl.BlockSpec(a.shape, lambda i: (0, 0))
    weight = pl.BlockSpec((features, tile), lambda i: (0, i))
    out = pl.BlockSpec((2 * rows, tile), lambda i: (0, i))
    return pl.pallas_call(
        functools.partial(project_kernel, rows, features),
        grid=(width // tile,),
        in_specs=[whole(own), whole(far), weight, weight],
        out_specs=[out, out],
        out_shape=[jax.ShapeDtypeStruct((2 * rows, width), F32)] * 2,
        scratch_shapes=[pltpu.VMEM((2 * rows, features), BF16)],
        compiler_params=pltpu.CompilerParams(vmem_limit_bytes=VMEM_BYTES),
        cost_estimate=pl.CostEstimate(
            flops=8 * rows * features * width,
            bytes_accessed=4 * features * width + 16 * rows * width,
            transcendentals=0,
        ),
    )(own, far, w0, w1)


def backward_kernel(
    rows, features, hidden, tile, split, experts_ref,
    g0_ref, u0_ref, g1_ref, u1_ref, own_ref, far_ref, meta_own, meta_far, d0_ref, d1_ref, w0_ref, w1_ref,
    out_own, out_far, both, grads, gates, weights,
):
    step = pl.program_id(0)
    lane = lax.broadcasted_iota(jnp.int32, (2 * rows, LANES), 1)

    @pl.when(step == 0)
    def _():
        both[:rows, :] = own_ref[...]
        both[rows:, :] = far_ref[...]
        weights[:rows, :] = meta_own[...].astype(F32)
        weights[rows:, :] = meta_far[...].astype(F32)
        gates[...] = jnp.zeros_like(gates)

    def first(expert, g_ref, u_ref, d_ref, base, part):
        gate_pre, up_pre = g_ref[...], u_ref[...]
        hidden_grad = lax.dot_general(both[...], d_ref[...], NT, preferred_element_type=F32)
        sigmoid = 1.0 / (1.0 + jnp.exp(-gate_pre))
        active = gate_pre * sigmoid
        here = lane == experts_ref[expert]
        scale = jnp.sum(jnp.where(here, weights[...], 0.0), axis=1, keepdims=True)
        total = jnp.sum(hidden_grad * active * up_pre, axis=1, keepdims=True)
        gates[...] += jnp.where(here, total, 0.0)
        scaled = scale * hidden_grad
        grads[:, pl.ds(base + part * tile, tile)] = (
            scaled * up_pre * sigmoid * (1.0 + gate_pre * (1.0 - sigmoid))
        ).astype(BF16)
        grads[:, pl.ds(base + hidden + part * tile, tile)] = (scaled * active).astype(BF16)

    parts = hidden // tile
    for part in range(parts):
        pl.when(step == part)(
            functools.partial(first, 0, g0_ref, u0_ref, d0_ref, 0, part)
        )
        pl.when(step == parts + part)(
            functools.partial(first, 1, g1_ref, u1_ref, d1_ref, 2 * hidden, part)
        )

    def second(part):
        out = lax.dot_general(grads[:, : 2 * hidden], w0_ref[...], NT, preferred_element_type=F32)
        out += lax.dot_general(grads[:, 2 * hidden :], w1_ref[...], NT, preferred_element_type=F32)
        out = out.astype(BF16)
        out_own[:, pl.ds(part * split, split)] = out[:rows]
        out_far[:, pl.ds(part * split, split)] = out[rows:]

    for part in range(features // split):
        pl.when(step == 2 * parts + part)(functools.partial(second, part))

    @pl.when(step == 2 * parts)
    def _():
        out_own[:, features:] = gates[:rows].astype(BF16)
        out_far[:, features:] = gates[rows:].astype(BF16)


def backward(experts, p0, p1, own, far, tok_own, tok_far, d0, d1, w0, w1, tile=384, split=256):
    rows, features = own.shape
    hidden = d0.shape[0]
    parts = hidden // tile
    steps = 2 * parts + features // split
    at0 = lambda i: jnp.minimum(i, parts - 1)
    at1 = lambda i: jnp.clip(i - parts, 0, parts - 1)
    late = lambda i: jnp.maximum(i - 2 * parts, 0)
    whole = lambda a: pl.BlockSpec(a.shape, lambda i, e: (0, 0))
    pre = lambda at, off: pl.BlockSpec((2 * rows, tile), lambda i, e: (0, at(i) + off))
    meta = pl.BlockSpec((rows, LANES), lambda i, e: (0, features // LANES))
    down = lambda at: pl.BlockSpec((tile, features), lambda i, e: (at(i), 0))
    weight = pl.BlockSpec((split, 2 * hidden), lambda i, e: (late(i), 0))
    out = pl.BlockSpec((rows, features + LANES), lambda i, e: (0, 0))
    return pl.pallas_call(
        functools.partial(backward_kernel, rows, features, hidden, tile, split),
        grid_spec=pltpu.PrefetchScalarGridSpec(
            num_scalar_prefetch=1,
            grid=(steps,),
            in_specs=[
                pre(at0, 0), pre(at0, parts), pre(at1, 0), pre(at1, parts),
                whole(own), whole(far), meta, meta, down(at0), down(at1), weight, weight,
            ],
            out_specs=[out, out],
            scratch_shapes=[
                pltpu.VMEM((2 * rows, features), BF16),
                pltpu.VMEM((2 * rows, 4 * hidden), BF16),
                pltpu.VMEM((2 * rows, LANES), F32),
                pltpu.VMEM((2 * rows, LANES), F32),
            ],
        ),
        out_shape=[jax.ShapeDtypeStruct((rows, features + LANES), BF16)] * 2,
        compiler_params=pltpu.CompilerParams(vmem_limit_bytes=VMEM_BYTES),
        cost_estimate=pl.CostEstimate(
            flops=24 * rows * features * hidden,
            bytes_accessed=12 * features * hidden + 32 * rows * hidden,
            transcendentals=4 * rows * hidden,
        ),
    )(experts, p0, p0, p1, p1, own, far, tok_own, tok_far, d0, d1, w0, w1)


def ring_shards(lines, tokens, cotangent, expert_ids, gate_weights, w_gate_up, w_down):
    devices = lax.axis_size("expert")
    depth = devices // (2 * lines)
    rows, features = tokens.shape
    index = lambda z, y, c: (z * lines + y) * 2 + c
    places = [(z, y, c) for z in range(depth) for y in range(lines) for c in range(2)]
    up = [(index(z, y, c), index((z + 1) % depth, y, c)) for z, y, c in places]
    across = [(index(z, y, c), index(z, 1 - y, c)) for z, y, c in places]
    twin = [(index(z, y, c), index(z, y, 1 - c)) for z, y, c in places]
    move = lambda a, pairs: lax.ppermute(a, "expert", pairs)

    me = lax.axis_index("expert")
    experts = jnp.stack([me, me ^ 1]).astype(jnp.int32)
    lane = jnp.arange(LANES, dtype=jnp.int32)
    at = expert_ids[:, :, None] == lane
    table = jnp.sum(jnp.where(at, gate_weights[:, :, None], 0), axis=1).astype(BF16)
    x = [jnp.concatenate([tokens, table], axis=1)]
    g = [cotangent]
    w0, d0 = w_gate_up[0], w_down[0]
    w1, d1 = move(w0, twin), move(d0, twin)
    for _ in range(depth - 1):
        x.append(move(x[-1], up))
        g.append(move(g[-1], up))
    xf = [move(a, across) for a in x]
    gf = [move(a, across) for a in g]
    mine, total = [], []
    for s in range(depth):
        p0, p1 = project(x[s], xf[s], w0, w1)
        own, far = backward(experts, p0, p1, g[s], gf[s], x[s], xf[s], d0, d1, w0, w1)
        mine.append((own, move(far, across)))
    for s in list(range(1, depth)) + [0]:
        own, back = mine[s]
        here = own.astype(F32) + back.astype(F32)
        if total:
            here = here + move(total[-1], up).astype(F32)
        total.append(here.astype(BF16))
    last = total[-1]
    picked = jnp.where(at, last[:, None, features:], 0)
    return last[:, :features], jnp.sum(picked, axis=2).astype(BF16)


def solution(mesh):
    row, cube = P(("parts", "expert"), None), P(("parts", "expert"), None, None)
    body = functools.partial(ring_shards, 2)
    return jax.shard_map(
        body, mesh=mesh, in_specs=(row, row, row, row, cube, cube), out_specs=(row, row), check_vma=False
    )
```

```python
import functools

import jax
import jax.numpy as jnp
from jax import lax
from jax.experimental import pallas as pl
from jax.experimental.pallas import tpu as pltpu
from jax.sharding import PartitionSpec as P

F32, BF16 = jnp.float32, jnp.bfloat16
LANES = 128
VMEM_BYTES = 16 * 2**20
COST = 30
NT = (((1,), (1,)), ((), ()))
LOCAL = pl.BlockSpec(memory_space=pltpu.VMEM)
SCALAR = pl.BlockSpec(memory_space=pltpu.SMEM)
ANYWHERE = pl.BlockSpec(memory_space=pl.ANY)


def resident(a):
    return pltpu.with_memory_space_constraint(a, pltpu.VMEM)


def call(kernel, ins, outs, scratch=(), flops=0):
    return pl.pallas_call(
        kernel,
        in_specs=ins,
        out_specs=[spec for spec, _ in outs],
        out_shape=[shape for _, shape in outs],
        scratch_shapes=list(scratch),
        compiler_params=pltpu.CompilerParams(vmem_limit_bytes=VMEM_BYTES),
        cost_estimate=pl.CostEstimate(flops=COST * flops // 100, bytes_accessed=1024, transcendentals=0),
    )


def array(*shape, dtype=BF16):
    return LOCAL, jax.ShapeDtypeStruct(shape, dtype)


def load_kernel(count, *refs):
    sems = refs[-1]
    copies = [pltpu.make_async_copy(refs[i], refs[count + i], sems.at[i]) for i in range(count)]
    for c in copies:
        c.start()
    for c in copies:
        c.wait()


def load(*arrays):
    n = len(arrays)
    return call(
        functools.partial(load_kernel, n), [ANYWHERE] * n, [array(*a.shape) for a in arrays],
        [pltpu.SemaphoreType.DMA((n,))],
    )(*arrays)


def choose_kernel(near, pair_ref, x_ref, _, out_ref, sel_ref, *same_ref):
    for ref in same_ref:
        ref[...] = x_ref[...]
    rows = x_ref.shape[0]
    table = x_ref[:, x_ref.shape[1] - LANES :].astype(F32)
    lane = lax.broadcasted_iota(jnp.int32, (8, LANES), 1)
    pick = jnp.where((lane == pair_ref[0]) | (lane == pair_ref[1]), 1.0, 0.0)
    named = jnp.where(table > 0.0, 1.0, 0.0)
    need = jnp.minimum(lax.dot_general(pick, named, NT, preferred_element_type=F32), 1.0)
    before = lax.broadcasted_iota(jnp.int32, (rows, rows), 0) < lax.broadcasted_iota(jnp.int32, (rows, rows), 1)
    place = jnp.dot(need, jnp.where(before, 1.0, 0.0), preferred_element_type=F32)
    slot = lax.broadcasted_iota(jnp.int32, (near, rows), 0)
    sel = jnp.where((place[:1].astype(jnp.int32) == slot) & (need[:1] > 0.0), 1.0, 0.0).astype(BF16)
    sel_ref[...] = sel
    out_ref[...] = jnp.dot(sel, x_ref[...], preferred_element_type=F32).astype(BF16)


def choose(pair, x, near, ticket, again):
    rows, width = x.shape
    return call(
        functools.partial(choose_kernel, near),
        [SCALAR, LOCAL, SCALAR],
        [array(near, width), array(near, rows)] + [array(*x.shape)] * again,
        flops=2 * near * rows * width,
    )(pair, resident(x), ticket)


def pack_kernel(sel_ref, g_ref, _, out_ref, *same_ref):
    for ref in same_ref:
        ref[...] = g_ref[...]
    out_ref[...] = jnp.dot(sel_ref[...], g_ref[...], preferred_element_type=F32).astype(BF16)


def pack(sel, g, ticket, again):
    near, rows = sel.shape
    width = g.shape[1]
    return call(
        pack_kernel, [LOCAL] * 2 + [SCALAR], [array(near, width)] + [array(*g.shape)] * again,
        flops=2 * near * rows * width,
    )(sel, resident(g), ticket)


def spread(sel_ref, back_ref, at):
    return lax.dot_general(
        sel_ref[...], back_ref[:, at], (((0,), (0,)), ((), ())), preferred_element_type=F32
    )


def gather_kernel(own_ref, back_ref, sel_ref, *refs):
    total = own_ref[...].astype(F32) + spread(sel_ref, back_ref, slice(None))
    if len(refs) > 1:
        total += refs[0][...].astype(F32)
    refs[-1][...] = total.astype(BF16)


def gather(own, back, sel, *carried):
    return call(
        gather_kernel, [LOCAL] * (3 + len(carried)), [array(*own.shape)], flops=2 * back.size * sel.shape[1]
    )(own, back, sel, *carried)[0]


def finish_kernel(own_ref, back_ref, sel_ref, carried_ref, ids_ref, out_ref, gates_ref):
    features = out_ref.shape[1]
    fanout = ids_ref.shape[1]
    total = own_ref[...].astype(F32) + spread(sel_ref, back_ref, slice(None)) + carried_ref[...].astype(F32)
    out_ref[...] = total[:, :features].astype(BF16)
    gates = total[:, features:]
    lane = lax.broadcasted_iota(jnp.int32, gates.shape, 1)
    column = lax.broadcasted_iota(jnp.int32, gates_ref.shape, 1)
    chosen = jnp.zeros(gates_ref.shape, F32)
    for k in range(fanout):
        value = jnp.sum(jnp.where(lane == ids_ref[:, k : k + 1], gates, 0.0), axis=1, keepdims=True)
        chosen = jnp.where(column == k, value, chosen)
    gates_ref[...] = chosen.astype(BF16)


def finish(own, back, sel, carried, ids):
    rows, width = own.shape
    return call(
        finish_kernel, [LOCAL] * 5, [array(rows, width - LANES), array(*ids.shape)],
        flops=2 * back.size * rows,
    )(own, back, sel, carried, ids)


def project_kernel(tile, ticket_ref, own_ref, far_ref, w0_ref, w1_ref, _, out0_ref, out1_ref, ticket_out, both):
    features, width = w0_ref.shape
    rows = own_ref.shape[0]
    both[:rows, :] = own_ref[:, :features]
    both[rows:, :] = far_ref[:, :features]
    for w_ref, out_ref in ((w0_ref, out0_ref), (w1_ref, out1_ref)):
        for j in range(width // tile):
            at = pl.ds(j * tile, tile)
            out_ref[:, at] = jnp.dot(both[...], w_ref[:, at], preferred_element_type=F32)
    for i in range(2):
        ticket_out[i] = ticket_ref[i]


def project(ticket, own, far, w0, w1, after, tile=512):
    rows = own.shape[0] + far.shape[0]
    features, width = w0.shape
    return call(
        functools.partial(project_kernel, tile),
        [SCALAR] + [LOCAL] * 4 + [ANYWHERE],
        [array(rows, width, dtype=F32)] * 2 + [(SCALAR, jax.ShapeDtypeStruct((2,), jnp.int32))],
        [pltpu.VMEM((rows, features), BF16)],
        flops=4 * rows * features * width,
    )(ticket, *map(resident, (own, far, w0, w1)), after)


def backward_kernel(
    tile, split, experts_ref, p0_ref, p1_ref, own_ref, far_ref, tok_own, tok_far, d0_ref, d1_ref, w0_ref, w1_ref,
    _, out_own, out_far, experts_out, both, meta, grads,
):
    hidden, features = d0_ref.shape
    parts, splits = hidden // tile, features // split
    rows = own_ref.shape[0]
    both[:rows, :] = own_ref[...]
    both[rows:, :] = far_ref[...]
    meta[:rows, :] = tok_own[:, features:].astype(F32)
    meta[rows:, :] = tok_far[:, features:].astype(F32)
    lane = lax.broadcasted_iota(jnp.int32, meta.shape, 1)
    gates = jnp.zeros(meta.shape, F32)
    for e, (p_ref, d_ref) in enumerate(((p0_ref, d0_ref), (p1_ref, d1_ref))):
        here = lane == experts_ref[e]
        scale = jnp.sum(jnp.where(here, meta[...], 0.0), axis=1, keepdims=True)
        total = jnp.zeros((meta.shape[0], 1), F32)
        for j in range(parts):
            hidden_grad = lax.dot_general(
                both[...], d_ref[pl.ds(j * tile, tile)], NT, preferred_element_type=F32
            )
            gate_pre = p_ref[:, pl.ds(j * tile, tile)]
            up_pre = p_ref[:, pl.ds(hidden + j * tile, tile)]
            sigmoid = 1.0 / (1.0 + jnp.exp(-gate_pre))
            active = gate_pre * sigmoid
            total += jnp.sum(hidden_grad * active * up_pre, axis=1, keepdims=True)
            scaled = scale * hidden_grad
            base = 2 * e * hidden + j * tile
            grads[:, pl.ds(base, tile)] = (
                scaled * up_pre * sigmoid * (1.0 + gate_pre * (1.0 - sigmoid))
            ).astype(BF16)
            grads[:, pl.ds(base + hidden, tile)] = (scaled * active).astype(BF16)
        gates += jnp.where(here, total, 0.0)
        experts_out[e] = experts_ref[e]
    out_own[:, features:] = gates[:rows].astype(BF16)
    out_far[:, features:] = gates[rows:].astype(BF16)
    for j in range(splits):
        at = pl.ds(j * split, split)
        out = lax.dot_general(grads[:, : 2 * hidden], w0_ref[at], NT, preferred_element_type=F32)
        out += lax.dot_general(grads[:, 2 * hidden :], w1_ref[at], NT, preferred_element_type=F32)
        out_own[:, at] = out[:rows].astype(BF16)
        out_far[:, at] = out[rows:].astype(BF16)


def backward(experts, p0, p1, own, far, tok_own, tok_far, d0, d1, w0, w1, after, tile=256, split=512):
    rows = own.shape[0] + far.shape[0]
    hidden, features = d0.shape
    return call(
        functools.partial(backward_kernel, tile, split),
        [SCALAR] + [LOCAL] * 10 + [ANYWHERE],
        [array(own.shape[0], features + LANES), array(far.shape[0], features + LANES)]
        + [(SCALAR, jax.ShapeDtypeStruct((2,), jnp.int32))],
        [pltpu.VMEM((rows, features), BF16), pltpu.VMEM((rows, LANES), F32), pltpu.VMEM((rows, 4 * hidden), BF16)],
        flops=12 * rows * features * hidden,
    )(experts, p0, p1, *map(resident, (own, far, tok_own, tok_far, d0, d1, w0, w1)), after)


def shards(lines, tokens, cotangent, expert_ids, gate_weights, w_gate_up, w_down):
    devices = lax.axis_size("expert")
    depth = devices // (2 * lines)
    rows, features = tokens.shape
    fanout = expert_ids.shape[1]
    capacity = 7 * rows * fanout // (4 * devices)
    near = min(rows, -(-2 * capacity // 16) * 16)
    index = lambda z, y, c: (z * lines + y) * 2 + c
    places = [(z, y, c) for z in range(depth) for y in range(lines) for c in range(2)]
    up = [(index(z, y, c), index((z + 1) % depth, y, c)) for z, y, c in places]
    across = [(index(z, y, c), index(z, 1 - y, c)) for z, y, c in places]
    twin = [(index(z, y, c), index(z, y, 1 - c)) for z, y, c in places]
    move = lambda a, pairs: lax.ppermute(a, "expert", pairs)

    me = lax.axis_index("expert")
    experts = jnp.stack([me, me ^ 1]).astype(jnp.int32)
    others = experts ^ 2
    at = expert_ids[:, :, None] == jnp.arange(LANES, dtype=jnp.int32)
    table = jnp.sum(jnp.where(at, gate_weights[:, :, None], 0), axis=1).astype(BF16)
    w0, d0 = w_gate_up[0], w_down[0]
    w1, d1 = move(w0, twin), move(d0, twin)
    w0, d0 = load(w0, d0)
    w1, d1 = load(w1, d1)
    x, g = jnp.concatenate([tokens, table], axis=1), cotangent
    nx, ng = move(x, up), move(g, up)
    xs, sel = choose(others, x, near, experts, False)
    gs, = pack(sel, g, experts, False)
    parts = []
    for s in range(depth):
        xf, gf = move(xs, across), move(gs, across)
        now = x, g, sel
        if s + 1 < depth:
            again = s + 2 < depth
            xs, sel, *kept = choose(others, nx, near, experts, again)
            x = kept[0] if again else nx
            if again:
                nx = move(x, up)
        p0, p1, experts = project(experts, now[0], xf, w0, w1, xs)
        if s + 1 < depth:
            gs, *kept = pack(sel, ng, experts, again)
            g = kept[0] if again else ng
            if again:
                ng = move(g, up)
        own, far, experts = backward(experts, p0, p1, now[1], gf, now[0], xf, d0, d1, w0, w1, gs)
        parts.append((own, move(far, across), now[2]))
    carried = ()
    for s in range(1, depth):
        carried = (move(gather(*parts[s], *carried), up),)
    return tuple(finish(*parts[0], *carried, expert_ids))


def solution(mesh):
    row, cube = P(("parts", "expert"), None), P(("parts", "expert"), None, None)
    body = functools.partial(shards, 2)
    return jax.shard_map(
        body, mesh=mesh, in_specs=(row, row, row, row, cube, cube), out_specs=(row, row), check_vma=False
    )
```

```python
import functools

import jax
import jax.numpy as jnp
from jax import lax
from jax.experimental import pallas as pl
from jax.experimental.pallas import tpu as pltpu
from jax.sharding import PartitionSpec as P

F32, BF16 = jnp.float32, jnp.bfloat16
LANES = 128
VMEM_BYTES = 16 * 2**20
COST = 30
HOLD = 8 * 10**9, 0, 8 * 10**9
NT = (((1,), (1,)), ((), ()))
LOCAL = pl.BlockSpec(memory_space=pltpu.VMEM)
SCALAR = pl.BlockSpec(memory_space=pltpu.SMEM)
ANYWHERE = pl.BlockSpec(memory_space=pl.ANY)


def array(*shape, dtype=BF16):
    return jax.ShapeDtypeStruct(shape, dtype)


class Queue:
    def __init__(self, ticket):
        self.ticket = ticket

    def run(self, kernel, operands, outs, scratch=(), flops=0, anywhere=0):
        def body(ticket_ref, *refs):
            n = len(operands) + len(outs)
            kernel(ticket_ref, *refs[:n], *refs[n + 1 :])
            for i in range(4):
                refs[n][i] = ticket_ref[i]

        *results, self.ticket = pl.pallas_call(
            body,
            in_specs=[SCALAR] + [ANYWHERE] * anywhere + [LOCAL] * (len(operands) - anywhere),
            out_specs=[LOCAL] * len(outs) + [SCALAR],
            out_shape=list(outs) + [array(4, dtype=jnp.int32)],
            scratch_shapes=list(scratch),
            compiler_params=pltpu.CompilerParams(vmem_limit_bytes=VMEM_BYTES),
            cost_estimate=pl.CostEstimate(flops=COST * flops // 100, bytes_accessed=0, transcendentals=0),
        )(self.ticket, *[pltpu.with_memory_space_constraint(a, pltpu.HBM if i < anywhere else pltpu.VMEM) for i, a in enumerate(operands)])
        return results[0] if len(results) == 1 else results


def load_kernel(count, pieces, _, *refs):
    sems = refs[-1]
    copies = []
    for i in range(count):
        rows = refs[i].shape[0] // pieces
        for j in range(pieces):
            at = pl.ds(j * rows, rows)
            copies.append(pltpu.make_async_copy(refs[i].at[at], refs[count + i].at[at], sems.at[i, j]))
            copies[-1].start()
    for c in copies:
        c.wait()


def load(queue, *arrays, pieces=4):
    n = len(arrays)
    return queue.run(
        functools.partial(load_kernel, n, pieces), arrays, [array(*a.shape) for a in arrays],
        [pltpu.SemaphoreType.DMA((n, pieces))], anywhere=n,
    )


def selection(table, ids_ref, near):
    rows = table.shape[0]
    lane = lax.broadcasted_iota(jnp.int32, (8, LANES), 1)
    pick = jnp.where((lane == ids_ref[2]) | (lane == ids_ref[3]), 1.0, 0.0)
    named = jnp.where(table > 0.0, 1.0, 0.0)
    need = jnp.minimum(lax.dot_general(pick, named, NT, preferred_element_type=F32), 1.0)
    before = lax.broadcasted_iota(jnp.int32, (rows, rows), 0) < lax.broadcasted_iota(jnp.int32, (rows, rows), 1)
    place = jnp.dot(need, jnp.where(before, 1.0, 0.0), preferred_element_type=F32)
    slot = lax.broadcasted_iota(jnp.int32, (near, rows), 0)
    return jnp.where((place[:1].astype(jnp.int32) == slot) & (need[:1] > 0.0), 1.0, 0.0).astype(BF16)


def choose_kernel(near, ids_ref, x_ref, out_ref, sel_ref, *same_ref):
    for ref in same_ref:
        ref[...] = x_ref[...]
    sel_ref[...] = selection(x_ref[:, x_ref.shape[1] - LANES :].astype(F32), ids_ref, near)
    out_ref[...] = jnp.dot(sel_ref[...], x_ref[...], preferred_element_type=F32).astype(BF16)


def choose(queue, x, near, again):
    rows, width = x.shape
    outs = [array(near, width), array(near, rows)] + [array(rows, width)] * again
    return queue.run(functools.partial(choose_kernel, near), [x], outs)


def prepare_kernel(near, ids_ref, tokens_ref, named_hbm, weight_hbm, x_ref, out_ref, sel_ref, named_ref, weight_ref, sems):
    rows, features = tokens_ref.shape
    copies = [
        pltpu.make_async_copy(named_hbm, named_ref, sems.at[0]),
        pltpu.make_async_copy(weight_hbm, weight_ref, sems.at[1]),
        pltpu.make_async_copy(tokens_ref, x_ref.at[:, pl.ds(0, features)], sems.at[2]),
    ]
    for c in copies:
        c.start()
    for c in copies[:2]:
        c.wait()
    expert = lax.broadcasted_iota(jnp.int32, (LANES, rows), 0)
    table = jnp.zeros((LANES, rows), F32)
    for k in range(named_ref.shape[0]):
        weight = weight_ref[k : k + 1, :].astype(F32)
        table += jnp.where(expert == named_ref[k : k + 1, :], weight, 0.0)
    row = lax.broadcasted_iota(jnp.int32, (LANES, rows), 1).astype(F32)
    table = jnp.where(expert == LANES - 1, row, table).T
    x_ref[:, features:] = table.astype(BF16)
    sel_ref[...] = selection(table, ids_ref, near)
    copies[2].wait()
    out_ref[...] = jnp.dot(sel_ref[...], x_ref[...], preferred_element_type=F32).astype(BF16)


def prepare(queue, tokens, ids, weights, near):
    rows, features = tokens.shape
    width = features + LANES
    return queue.run(
        functools.partial(prepare_kernel, near),
        [tokens, ids, weights],
        [array(rows, width), array(near, width), array(near, rows)],
        [pltpu.VMEM(ids.shape, jnp.int32), pltpu.VMEM(weights.shape, BF16), pltpu.SemaphoreType.DMA((3,))],
        anywhere=3,
    )


def pack_kernel(_, sel_ref, g_ref, out_ref, *same_ref):
    for ref in same_ref:
        ref[...] = g_ref[...]
    out_ref[...] = jnp.dot(sel_ref[...], g_ref[...], preferred_element_type=F32).astype(BF16)


def pack(queue, sel, g, again):
    outs = [array(sel.shape[0], g.shape[1])] + [array(*g.shape)] * again
    return queue.run(pack_kernel, [sel, g], outs)


def spread(sel_ref, back_ref):
    return lax.dot_general(
        sel_ref[...], back_ref[...], (((0,), (0,)), ((), ())), preferred_element_type=F32
    )


def place_kernel(cuts, _, far_ref, tok_ref, *refs):
    near, width = far_ref.shape
    rows = refs[-1].shape[0]
    row = tok_ref[:, width - 1 :].astype(F32).astype(jnp.int32)
    sel = jnp.where(lax.broadcasted_iota(jnp.int32, (near, rows), 1) == row, 1.0, 0.0).astype(BF16)
    total = lax.dot_general(sel, far_ref[...], (((0,), (0,)), ((), ())), preferred_element_type=F32)
    for ref in refs[: -len(cuts)]:
        total += ref[...].astype(F32)
    for (at, end), ref in zip(cuts, refs[-len(cuts) :]):
        ref[...] = total[:, at:end].astype(BF16)


def place(queue, far, tok, rows, *carried, cuts=None):
    cuts = cuts or [(0, far.shape[1])]
    outs = [array(rows, end - at) for at, end in cuts]
    return queue.run(functools.partial(place_kernel, cuts), [far, tok, *carried], outs)


def gather_kernel(cut, _, own_ref, back_ref, sel_ref, *refs):
    at, end = cut
    total = own_ref[:, at:end].astype(F32) + spread(sel_ref, back_ref)
    for ref in refs[:-1]:
        total += (ref[...] if ref.shape == total.shape else ref[:, at:end]).astype(F32)
    refs[-1][...] = total.astype(BF16)


def gather(queue, own, back, sel, cut, *carried, flops=0):
    return queue.run(
        functools.partial(gather_kernel, cut), [own, back, sel, *carried],
        [array(own.shape[0], cut[1] - cut[0])], flops=flops,
    )


def add_kernel(cut, kept, _, *refs):
    for ref, same_ref in zip(refs[:kept], refs[len(refs) - kept :]):
        same_ref[...] = ref[...]
    *block_refs, out_ref = refs[kept : len(refs) - kept]
    width = out_ref.shape[1]
    blocks = [ref[...] if ref.shape[1] == width else ref[:, cut[0] : cut[1]] for ref in block_refs]
    out_ref[...] = sum(block.astype(F32) for block in blocks).astype(BF16)


def add(queue, cut, *blocks, kept=()):
    outs = [array(blocks[0].shape[0], cut[1] - cut[0])] + [array(*a.shape) for a in kept]
    return queue.run(functools.partial(add_kernel, cut, len(kept)), [*kept, *blocks], outs)


def total(own_ref, back_ref, sel_ref, carried_ref, at):
    end = at + carried_ref.shape[1]
    return own_ref[:, at:end].astype(F32) + spread(sel_ref, back_ref.at[:, pl.ds(at, end - at)]) + carried_ref[...].astype(F32)


def front_kernel(_, own_ref, back_ref, sel_ref, carried_ref, out_ref):
    out_ref[...] = total(own_ref, back_ref, sel_ref, carried_ref, 0).astype(BF16)


def finish_kernel(_, own_ref, back_ref, sel_ref, carried_ref, front_ref, ids_ref, out_ref, gates_ref):
    features = out_ref.shape[1]
    at = front_ref.shape[1]
    out_ref[:, :at] = front_ref[...]
    rest = total(own_ref, back_ref, sel_ref, carried_ref, at)
    out_ref[:, at:] = rest[:, : features - at].astype(BF16)
    gates = rest[:, features - at :].T
    expert = lax.broadcasted_iota(jnp.int32, gates.shape, 0)
    for k in range(ids_ref.shape[0]):
        gates_ref[k : k + 1, :] = jnp.sum(jnp.where(expert == ids_ref[k : k + 1, :], gates, 0.0), axis=0, keepdims=True)


def finish(queue, own, back, sel, ids, first, second):
    rows, width = own.shape
    front = queue.run(front_kernel, [own, back, sel, first], [array(*first.shape)], flops=HOLD[2])
    return queue.run(
        finish_kernel, [own, back, sel, second, front, ids],
        [array(rows, width - LANES), array(*ids.shape, dtype=F32)],
    )


def project_kernel(tile, _, own_ref, far_ref, w0_ref, w1_ref, *refs):
    kept = (len(refs) - 3) // 2
    out0_ref, out1_ref = refs[kept : kept + 2]
    both = refs[-1]
    for ref, same_ref in zip(refs[:kept], refs[kept + 2 : -1]):
        same_ref[...] = ref[...]
    features, width = w0_ref.shape
    rows = own_ref.shape[0]
    both[:rows, :] = own_ref[:, :features]
    both[rows:, :] = far_ref[:, :features]
    for w_ref, out_ref in ((w0_ref, out0_ref), (w1_ref, out1_ref)):
        for j in range(width // tile):
            at = pl.ds(j * tile, tile)
            out_ref[:, at] = jnp.dot(both[...], w_ref[:, at], preferred_element_type=F32)


def project(queue, own, far, w0, w1, *kept, tile=512):
    rows = own.shape[0] + far.shape[0]
    features, width = w0.shape
    return queue.run(
        functools.partial(project_kernel, tile),
        [own, far, w0, w1, *kept],
        [array(rows, width, dtype=F32)] * 2 + [array(*a.shape) for a in kept],
        [pltpu.VMEM((rows, features), BF16)],
        flops=4 * rows * features * width,
    )


def backward_kernel(
    tile, split, ids_ref, p0_ref, p1_ref, own_ref, far_ref, tok_own, tok_far, d0_ref, d1_ref, w0_ref, w1_ref,
    out_own, *refs,
):
    hidden, features = d0_ref.shape
    parts, splits = hidden // tile, features // split
    rows = own_ref.shape[0]
    *out_fars, both, meta, grads = refs
    starts = [sum(ref.shape[1] for ref in out_fars[:i]) for i in range(len(out_fars))]
    both[:rows, :] = own_ref[...]
    both[rows:, :] = far_ref[...]
    meta[:rows, :] = tok_own[:, features:].astype(F32)
    meta[rows:, :] = tok_far[:, features:].astype(F32)
    lane = lax.broadcasted_iota(jnp.int32, meta.shape, 1)
    gates = jnp.zeros(meta.shape, F32)
    for e, (p_ref, d_ref) in enumerate(((p0_ref, d0_ref), (p1_ref, d1_ref))):
        here = lane == ids_ref[e]
        scale = jnp.sum(jnp.where(here, meta[...], 0.0), axis=1, keepdims=True)
        total = jnp.zeros((meta.shape[0], 1), F32)
        for j in range(parts):
            at = pl.ds(j * tile, tile)
            hidden_grad = lax.dot_general(both[...], d_ref[at], NT, preferred_element_type=F32)
            gate_pre = p_ref[:, at]
            up_pre = p_ref[:, pl.ds(hidden + j * tile, tile)]
            sigmoid = 1.0 / (1.0 + jnp.exp(-gate_pre))
            active = gate_pre * sigmoid
            total += jnp.sum(hidden_grad * active * up_pre, axis=1, keepdims=True)
            scaled = scale * hidden_grad
            base = 2 * e * hidden + j * tile
            grads[:, pl.ds(base, tile)] = (
                scaled * up_pre * sigmoid * (1.0 + gate_pre * (1.0 - sigmoid))
            ).astype(BF16)
            grads[:, pl.ds(base + hidden, tile)] = (scaled * active).astype(BF16)
        gates += jnp.where(here, total, 0.0)
    out_own[:, features:] = gates[:rows].astype(BF16)
    out_fars[-1][:, features - starts[-1] :] = gates[rows:].astype(BF16)
    for j in range(splits):
        at = pl.ds(j * split, split)
        out = lax.dot_general(grads[:, : 2 * hidden], w0_ref[at], NT, preferred_element_type=F32)
        out += lax.dot_general(grads[:, 2 * hidden :], w1_ref[at], NT, preferred_element_type=F32)
        out_own[:, at] = out[:rows].astype(BF16)
        i = sum(start <= j * split for start in starts) - 1
        out_fars[i][:, pl.ds(j * split - starts[i], split)] = out[rows:].astype(BF16)


def backward(queue, p0, p1, own, far, tok_own, tok_far, d0, d1, w0, w1, cuts, tile=256, split=512):
    rows = own.shape[0] + far.shape[0]
    hidden, features = d0.shape
    return queue.run(
        functools.partial(backward_kernel, tile, split),
        [p0, p1, own, far, tok_own, tok_far, d0, d1, w0, w1],
        [array(own.shape[0], features + LANES)] + [array(far.shape[0], end - at) for at, end in cuts],
        [pltpu.VMEM((rows, features), BF16), pltpu.VMEM((rows, LANES), F32), pltpu.VMEM((rows, 4 * hidden), BF16)],
        flops=12 * rows * features * hidden,
    )


def shards(lines, tokens, cotangent, expert_ids, gate_weights, w_gate_up, w_down):
    devices = lax.axis_size("expert")
    depth = devices // (2 * lines)
    rows, features = tokens.shape
    fanout = expert_ids.shape[1]
    capacity = 7 * rows * fanout // (4 * devices)
    near = min(rows, -(-2 * capacity // 16) * 16)
    index = lambda z, y, c: (z * lines + y) * 2 + c
    places = [(z, y, c) for z in range(depth) for y in range(lines) for c in range(2)]
    up = [(index(z, y, c), index((z + 1) % depth, y, c)) for z, y, c in places]
    across = [(index(z, y, c), index(z, 1 - y, c)) for z, y, c in places]
    twin = [(index(z, y, c), index(z, y, 1 - c)) for z, y, c in places]
    move = lambda a, pairs: lax.ppermute(a, "expert", pairs)

    me = lax.axis_index("expert")
    queue = Queue(jnp.stack([me, me ^ 1, me ^ 2, me ^ 3]).astype(jnp.int32))
    ids, weights = expert_ids.T, gate_weights.T
    w0, d0 = w_gate_up[0], w_down[0]
    w1, d1 = move(w0, twin), move(d0, twin)
    last = depth - 1
    xs, gs, sels, xf, gf = [], [], [], [], []
    own, far, back = [], [], []
    early = 1 if depth == 4 else depth
    whole = [(0, features + LANES)]
    halves = [(0, features // 2), (features // 2, features + LANES)]
    nx = ng = None

    def take_tokens(s):
        nonlocal nx
        if s:
            x, again = nx, s < last
            packed, sel, *kept = choose(queue, x, near, again)
        else:
            x, packed, sel = prepare(queue, tokens, ids, weights, near)
            again = False
        x = kept[0] if again else x
        if s < last:
            nx = move(x, up)
        xf.append(move(packed, across))
        sels.append(sel)
        xs.append(x)

    def take_grads(s):
        nonlocal ng
        g, again = ng if s else cotangent, 0 < s < last
        packed = pack(queue, sels[s], g, again)
        if again:
            packed, g = packed
        if s < last:
            ng = move(g, up)
        gf.append(move(packed, across))
        gs.append(g)

    take_tokens(0)
    take_grads(0)
    w0, d0 = load(queue, w0, d0)
    w1, d1 = load(queue, w1, d1)
    take_tokens(1)
    for s in range(depth):
        if s == 1:
            take_tokens(2)
        kept = own[early : early + 1] if s == early + 2 else []
        p0, p1, *kept = project(queue, xs[s], xf[s], w0, w1, *kept)
        own[early : early + len(kept)] = kept
        if 1 < s < last:
            take_tokens(s + 1)
        if s == early + 1:
            lifted = move(place(queue, far[early], xf[early], rows), up)
        if s == early + 2:
            lifted = place(queue, far[s - 1], xf[s - 1], rows, lifted, cuts=halves)
            back[s - 1] = [move(a, across) for a in lifted]
        if s < 2:
            take_grads(s + 1)
        cuts = halves if s == last else whole
        mine, *other = backward(queue, p0, p1, gs[s], gf[s], xs[s], xf[s], d0, d1, w0, w1, cuts)
        if 1 < s < last:
            take_grads(s + 1)
        own.append(mine)
        far.append(other[0])
        back.append(None if s in (0, early, early + 1) else [move(a, across) for a in other])
    carried = [move(own[1] if early == 1 else gather(queue, own[1], back[1][0], sels[1], *whole), up)]
    for s in range(2, depth):
        if s == early + 1:
            first = add(queue, halves[0], own[s], back[s][0], *carried)
            second, later = add(queue, halves[1], own[s], back[s][1], *carried, kept=[far[0]])
            back[0] = move(later, across)
            carried = [first, second]
        elif s < last:
            carried = [gather(queue, own[s], back[s][0], sels[s], whole[0], *carried)]
        else:
            if len(carried) == 1:
                carried, back[0] = carried * 2, move(far[0], across)
            carried = [
                gather(queue, own[s], part, sels[s], cut, before, flops=cost)
                for cut, part, before, cost in zip(halves, back[s], carried, HOLD)
            ]
        carried = [move(a, up) for a in carried]
    grad_tokens, grad_gates = finish(queue, own[0], back[0], sels[0], ids, *carried)
    return grad_tokens, grad_gates.T.astype(BF16)


def solution(mesh):
    row, cube = P(("parts", "expert"), None), P(("parts", "expert"), None, None)
    body = functools.partial(shards, 2)
    return jax.shard_map(
        body, mesh=mesh, in_specs=(row, row, row, row, cube, cube), out_specs=(row, row), check_vma=False
    )
```

```python
import functools

import jax
import jax.numpy as jnp
from jax import lax
from jax.experimental import pallas as pl
from jax.experimental.pallas import tpu as pltpu
from jax.sharding import PartitionSpec as P

F32, BF16 = jnp.float32, jnp.bfloat16
LANES = 128
VMEM_BYTES = 16 * 2**20
COST = 30
HOLD = 8 * 10**9, 0, 8 * 10**9
NT = (((1,), (1,)), ((), ()))
LOCAL = pl.BlockSpec(memory_space=pltpu.VMEM)
SCALAR = pl.BlockSpec(memory_space=pltpu.SMEM)
ANYWHERE = pl.BlockSpec(memory_space=pl.ANY)


def array(*shape, dtype=BF16):
    return jax.ShapeDtypeStruct(shape, dtype)


class Queue:
    def __init__(self, ticket):
        self.ticket = ticket

    def run(self, kernel, operands, outs, scratch=(), flops=0, anywhere=0):
        def body(ticket_ref, *refs):
            n = len(operands) + len(outs)
            kernel(ticket_ref, *refs[:n], *refs[n + 1 :])
            for i in range(4):
                refs[n][i] = ticket_ref[i]

        *results, self.ticket = pl.pallas_call(
            body,
            in_specs=[SCALAR] + [ANYWHERE] * anywhere + [LOCAL] * (len(operands) - anywhere),
            out_specs=[LOCAL] * len(outs) + [SCALAR],
            out_shape=list(outs) + [array(4, dtype=jnp.int32)],
            scratch_shapes=list(scratch),
            compiler_params=pltpu.CompilerParams(vmem_limit_bytes=VMEM_BYTES),
            cost_estimate=pl.CostEstimate(flops=COST * flops // 100, bytes_accessed=0, transcendentals=0),
        )(self.ticket, *[pltpu.with_memory_space_constraint(a, pltpu.HBM if i < anywhere else pltpu.VMEM) for i, a in enumerate(operands)])
        return results[0] if len(results) == 1 else results


def load_kernel(count, pieces, _, *refs):
    sems = refs[-1]
    copies = []
    for i in range(count):
        rows = refs[i].shape[0] // pieces
        for j in range(pieces):
            at = pl.ds(j * rows, rows)
            copies.append(pltpu.make_async_copy(refs[i].at[at], refs[count + i].at[at], sems.at[i, j]))
            copies[-1].start()
    for c in copies:
        c.wait()


def load(queue, *arrays, pieces=4):
    n = len(arrays)
    return queue.run(
        functools.partial(load_kernel, n, pieces), arrays, [array(*a.shape) for a in arrays],
        [pltpu.SemaphoreType.DMA((n, pieces))], anywhere=n,
    )


def selection(table, ids_ref, near):
    rows = table.shape[0]
    lane = lax.broadcasted_iota(jnp.int32, (8, LANES), 1)
    pick = jnp.where((lane == ids_ref[2]) | (lane == ids_ref[3]), 1.0, 0.0)
    named = jnp.where(table > 0.0, 1.0, 0.0)
    need = jnp.minimum(lax.dot_general(pick, named, NT, preferred_element_type=F32), 1.0)
    before = lax.broadcasted_iota(jnp.int32, (rows, rows), 0) < lax.broadcasted_iota(jnp.int32, (rows, rows), 1)
    place = jnp.dot(need, jnp.where(before, 1.0, 0.0), preferred_element_type=F32)
    slot = lax.broadcasted_iota(jnp.int32, (near, rows), 0)
    return jnp.where((place[:1].astype(jnp.int32) == slot) & (need[:1] > 0.0), 1.0, 0.0).astype(BF16)


def choose_kernel(near, ids_ref, x_ref, out_ref, sel_ref, *same_ref):
    for ref in same_ref:
        ref[...] = x_ref[...]
    sel_ref[...] = selection(x_ref[:, x_ref.shape[1] - LANES :].astype(F32), ids_ref, near)
    out_ref[...] = jnp.dot(sel_ref[...], x_ref[...], preferred_element_type=F32).astype(BF16)


def choose(queue, x, near, again):
    rows, width = x.shape
    outs = [array(near, width), array(near, rows)] + [array(rows, width)] * again
    return queue.run(functools.partial(choose_kernel, near), [x], outs)


def prepare_kernel(near, ids_ref, tokens_ref, named_hbm, weight_hbm, x_ref, out_ref, sel_ref, named_ref, weight_ref, sems):
    rows, features = tokens_ref.shape
    copies = [
        pltpu.make_async_copy(named_hbm, named_ref, sems.at[0]),
        pltpu.make_async_copy(weight_hbm, weight_ref, sems.at[1]),
        pltpu.make_async_copy(tokens_ref, x_ref.at[:, pl.ds(0, features)], sems.at[2]),
    ]
    for c in copies:
        c.start()
    for c in copies[:2]:
        c.wait()
    expert = lax.broadcasted_iota(jnp.int32, (LANES, rows), 0)
    table = jnp.zeros((LANES, rows), F32)
    for k in range(named_ref.shape[0]):
        weight = weight_ref[k : k + 1, :].astype(F32)
        table += jnp.where(expert == named_ref[k : k + 1, :], weight, 0.0)
    row = lax.broadcasted_iota(jnp.int32, (LANES, rows), 1).astype(F32)
    table = jnp.where(expert == LANES - 1, row, table).T
    x_ref[:, features:] = table.astype(BF16)
    sel_ref[...] = selection(table, ids_ref, near)
    copies[2].wait()
    out_ref[...] = jnp.dot(sel_ref[...], x_ref[...], preferred_element_type=F32).astype(BF16)


def prepare(queue, tokens, ids, weights, near):
    rows, features = tokens.shape
    width = features + LANES
    return queue.run(
        functools.partial(prepare_kernel, near),
        [tokens, ids, weights],
        [array(rows, width), array(near, width), array(near, rows)],
        [pltpu.VMEM(ids.shape, jnp.int32), pltpu.VMEM(weights.shape, BF16), pltpu.SemaphoreType.DMA((3,))],
        anywhere=3,
    )


def pack_kernel(_, sel_ref, g_ref, out_ref, *same_ref):
    for ref in same_ref:
        ref[...] = g_ref[...]
    out_ref[...] = jnp.dot(sel_ref[...], g_ref[...], preferred_element_type=F32).astype(BF16)


def pack(queue, sel, g, again):
    outs = [array(sel.shape[0], g.shape[1])] + [array(*g.shape)] * again
    return queue.run(pack_kernel, [sel, g], outs)


def spread(sel_ref, back_ref):
    return lax.dot_general(
        sel_ref[...], back_ref[...], (((0,), (0,)), ((), ())), preferred_element_type=F32
    )


def place_kernel(cuts, _, far_ref, tok_ref, *refs):
    near, width = far_ref.shape
    rows = refs[-1].shape[0]
    row = tok_ref[:, width - 1 :].astype(F32).astype(jnp.int32)
    sel = jnp.where(lax.broadcasted_iota(jnp.int32, (near, rows), 1) == row, 1.0, 0.0).astype(BF16)
    total = lax.dot_general(sel, far_ref[...], (((0,), (0,)), ((), ())), preferred_element_type=F32)
    for ref in refs[: -len(cuts)]:
        total += ref[...].astype(F32)
    for (at, end), ref in zip(cuts, refs[-len(cuts) :]):
        ref[...] = total[:, at:end].astype(BF16)


def place(queue, far, tok, rows, *carried, cuts=None):
    cuts = cuts or [(0, far.shape[1])]
    outs = [array(rows, end - at) for at, end in cuts]
    return queue.run(functools.partial(place_kernel, cuts), [far, tok, *carried], outs)


def gather_kernel(cut, _, own_ref, back_ref, sel_ref, *refs):
    at, end = cut
    total = own_ref[:, at:end].astype(F32) + spread(sel_ref, back_ref)
    for ref in refs[:-1]:
        total += (ref[...] if ref.shape == total.shape else ref[:, at:end]).astype(F32)
    refs[-1][...] = total.astype(BF16)


def gather(queue, own, back, sel, cut, *carried, flops=0):
    return queue.run(
        functools.partial(gather_kernel, cut), [own, back, sel, *carried],
        [array(own.shape[0], cut[1] - cut[0])], flops=flops,
    )


def add_kernel(cut, kept, _, *refs):
    for ref, same_ref in zip(refs[:kept], refs[len(refs) - kept :]):
        same_ref[...] = ref[...]
    *block_refs, out_ref = refs[kept : len(refs) - kept]
    width = out_ref.shape[1]
    blocks = [ref[...] if ref.shape[1] == width else ref[:, cut[0] : cut[1]] for ref in block_refs]
    out_ref[...] = sum(block.astype(F32) for block in blocks).astype(BF16)


def add(queue, cut, *blocks, kept=()):
    outs = [array(blocks[0].shape[0], cut[1] - cut[0])] + [array(*a.shape) for a in kept]
    return queue.run(functools.partial(add_kernel, cut, len(kept)), [*kept, *blocks], outs)


def total(own_ref, back_ref, sel_ref, carried_ref, at):
    end = at + carried_ref.shape[1]
    return own_ref[:, at:end].astype(F32) + spread(sel_ref, back_ref.at[:, pl.ds(at, end - at)]) + carried_ref[...].astype(F32)


def front_kernel(_, own_ref, back_ref, sel_ref, carried_ref, out_ref):
    out_ref[...] = total(own_ref, back_ref, sel_ref, carried_ref, 0).astype(BF16)


def finish_kernel(_, own_ref, back_ref, sel_ref, carried_ref, front_ref, ids_ref, out_ref, gates_ref):
    features = out_ref.shape[1]
    at = front_ref.shape[1]
    out_ref[:, :at] = front_ref[...]
    rest = total(own_ref, back_ref, sel_ref, carried_ref, at)
    out_ref[:, at:] = rest[:, : features - at].astype(BF16)
    gates = rest[:, features - at :].T
    expert = lax.broadcasted_iota(jnp.int32, gates.shape, 0)
    chosen = [
        jnp.sum(jnp.where(expert == ids_ref[k : k + 1, :], gates, 0.0), axis=0, keepdims=True)
        for k in range(ids_ref.shape[0])
    ]
    gates_ref[...] = jnp.concatenate(chosen, axis=0).astype(BF16)


def finish(queue, own, back, sel, ids, first, second):
    rows, width = own.shape
    front = queue.run(front_kernel, [own, back, sel, first], [array(*first.shape)], flops=HOLD[2])
    return queue.run(
        finish_kernel, [own, back, sel, second, front, ids],
        [array(rows, width - LANES), array(*ids.shape)],
    )


def project_kernel(tile, _, own_ref, far_ref, w0_ref, w1_ref, *refs):
    kept = (len(refs) - 3) // 2
    out0_ref, out1_ref = refs[kept : kept + 2]
    both = refs[-1]
    for ref, same_ref in zip(refs[:kept], refs[kept + 2 : -1]):
        same_ref[...] = ref[...]
    features, width = w0_ref.shape
    rows = own_ref.shape[0]
    both[:rows, :] = own_ref[:, :features]
    both[rows:, :] = far_ref[:, :features]
    for w_ref, out_ref in ((w0_ref, out0_ref), (w1_ref, out1_ref)):
        for j in range(width // tile):
            at = pl.ds(j * tile, tile)
            out_ref[:, at] = jnp.dot(both[...], w_ref[:, at], preferred_element_type=F32)


def project(queue, own, far, w0, w1, *kept, tile=512):
    rows = own.shape[0] + far.shape[0]
    features, width = w0.shape
    return queue.run(
        functools.partial(project_kernel, tile),
        [own, far, w0, w1, *kept],
        [array(rows, width, dtype=F32)] * 2 + [array(*a.shape) for a in kept],
        [pltpu.VMEM((rows, features), BF16)],
        flops=4 * rows * features * width,
    )


def backward_kernel(
    tile, split, ids_ref, p0_ref, p1_ref, own_ref, far_ref, tok_own, tok_far, d0_ref, d1_ref, w0_ref, w1_ref,
    out_own, *refs,
):
    hidden, features = d0_ref.shape
    parts, splits = hidden // tile, features // split
    rows = own_ref.shape[0]
    *out_fars, both, meta, grads = refs
    starts = [sum(ref.shape[1] for ref in out_fars[:i]) for i in range(len(out_fars))]
    both[:rows, :] = own_ref[...]
    both[rows:, :] = far_ref[...]
    meta[:rows, :] = tok_own[:, features:].astype(F32)
    meta[rows:, :] = tok_far[:, features:].astype(F32)
    lane = lax.broadcasted_iota(jnp.int32, meta.shape, 1)
    gates = jnp.zeros(meta.shape, F32)
    for e, (p_ref, d_ref) in enumerate(((p0_ref, d0_ref), (p1_ref, d1_ref))):
        here = lane == ids_ref[e]
        scale = jnp.sum(jnp.where(here, meta[...], 0.0), axis=1, keepdims=True)
        total = jnp.zeros((meta.shape[0], 1), F32)
        for j in range(parts):
            at = pl.ds(j * tile, tile)
            hidden_grad = lax.dot_general(both[...], d_ref[at], NT, preferred_element_type=F32)
            gate_pre = p_ref[:, at]
            up_pre = p_ref[:, pl.ds(hidden + j * tile, tile)]
            sigmoid = 1.0 / (1.0 + jnp.exp(-gate_pre))
            active = gate_pre * sigmoid
            total += jnp.sum(hidden_grad * active * up_pre, axis=1, keepdims=True)
            scaled = scale * hidden_grad
            base = 2 * e * hidden + j * tile
            grads[:, pl.ds(base, tile)] = (
                scaled * up_pre * sigmoid * (1.0 + gate_pre * (1.0 - sigmoid))
            ).astype(BF16)
            grads[:, pl.ds(base + hidden, tile)] = (scaled * active).astype(BF16)
        gates += jnp.where(here, total, 0.0)
    out_own[:, features:] = gates[:rows].astype(BF16)
    out_fars[-1][:, features - starts[-1] :] = gates[rows:].astype(BF16)
    for j in range(splits):
        at = pl.ds(j * split, split)
        out = lax.dot_general(grads[:, : 2 * hidden], w0_ref[at], NT, preferred_element_type=F32)
        out += lax.dot_general(grads[:, 2 * hidden :], w1_ref[at], NT, preferred_element_type=F32)
        out_own[:, at] = out[:rows].astype(BF16)
        i = sum(start <= j * split for start in starts) - 1
        out_fars[i][:, pl.ds(j * split - starts[i], split)] = out[rows:].astype(BF16)


def backward(queue, p0, p1, own, far, tok_own, tok_far, d0, d1, w0, w1, cuts, tile=256, split=512):
    rows = own.shape[0] + far.shape[0]
    hidden, features = d0.shape
    return queue.run(
        functools.partial(backward_kernel, tile, split),
        [p0, p1, own, far, tok_own, tok_far, d0, d1, w0, w1],
        [array(own.shape[0], features + LANES)] + [array(far.shape[0], end - at) for at, end in cuts],
        [pltpu.VMEM((rows, features), BF16), pltpu.VMEM((rows, LANES), F32), pltpu.VMEM((rows, 4 * hidden), BF16)],
        flops=12 * rows * features * hidden,
    )


def shards(lines, tokens, cotangent, expert_ids, gate_weights, w_gate_up, w_down):
    devices = lax.axis_size("expert")
    depth = devices // (2 * lines)
    rows, features = tokens.shape
    fanout = expert_ids.shape[1]
    capacity = 7 * rows * fanout // (4 * devices)
    near = min(rows, -(-2 * capacity // 16) * 16)
    index = lambda z, y, c: (z * lines + y) * 2 + c
    places = [(z, y, c) for z in range(depth) for y in range(lines) for c in range(2)]
    up = [(index(z, y, c), index((z + 1) % depth, y, c)) for z, y, c in places]
    across = [(index(z, y, c), index(z, 1 - y, c)) for z, y, c in places]
    twin = [(index(z, y, c), index(z, y, 1 - c)) for z, y, c in places]
    move = lambda a, pairs: lax.ppermute(a, "expert", pairs)

    me = lax.axis_index("expert")
    queue = Queue(jnp.stack([me, me ^ 1, me ^ 2, me ^ 3]).astype(jnp.int32))
    ids, weights = expert_ids.T, gate_weights.T
    w0, d0 = w_gate_up[0], w_down[0]
    w1, d1 = move(w0, twin), move(d0, twin)
    last = depth - 1
    xs, gs, sels, xf, gf = [], [], [], [], []
    own, far, back = [], [], []
    early = 1 if depth == 4 else depth
    whole = [(0, features + LANES)]
    halves = [(0, features // 2), (features // 2, features + LANES)]
    nx = ng = None

    def take_tokens(s):
        nonlocal nx
        if s:
            x, again = nx, s < last
            packed, sel, *kept = choose(queue, x, near, again)
        else:
            x, packed, sel = prepare(queue, tokens, ids, weights, near)
            again = False
        x = kept[0] if again else x
        if s < last:
            nx = move(x, up)
        xf.append(move(packed, across))
        sels.append(sel)
        xs.append(x)

    def take_grads(s):
        nonlocal ng
        g, again = ng if s else cotangent, 0 < s < last
        packed = pack(queue, sels[s], g, again)
        if again:
            packed, g = packed
        if s < last:
            ng = move(g, up)
        gf.append(move(packed, across))
        gs.append(g)

    take_tokens(0)
    w0, d0 = load(queue, w0, d0)
    take_grads(0)
    w1, d1 = load(queue, w1, d1)
    take_tokens(1)
    for s in range(depth):
        if s == 1:
            take_tokens(2)
        kept = own[early : early + 1] if s == early + 2 else []
        p0, p1, *kept = project(queue, xs[s], xf[s], w0, w1, *kept)
        own[early : early + len(kept)] = kept
        if 1 < s < last:
            take_tokens(s + 1)
        if s == early + 1:
            lifted = move(place(queue, far[early], xf[early], rows), up)
        if s == early + 2:
            lifted = place(queue, far[s - 1], xf[s - 1], rows, lifted, cuts=halves)
            back[s - 1] = [move(a, across) for a in lifted]
        if s == 0:
            take_grads(1)
        cuts = halves if s == last else whole
        mine, *other = backward(queue, p0, p1, gs[s], gf[s], xs[s], xf[s], d0, d1, w0, w1, cuts)
        if 0 < s < last:
            take_grads(s + 1)
        own.append(mine)
        far.append(other[0])
        back.append(None if s in (0, early, early + 1) else [move(a, across) for a in other])
    carried = [move(own[1] if early == 1 else gather(queue, own[1], back[1][0], sels[1], *whole), up)]
    for s in range(2, depth):
        if s == early + 1:
            first = add(queue, halves[0], own[s], back[s][0], *carried)
            second, later = add(queue, halves[1], own[s], back[s][1], *carried, kept=[far[0]])
            back[0] = move(later, across)
            carried = [first, second]
        elif s < last:
            carried = [gather(queue, own[s], back[s][0], sels[s], whole[0], *carried)]
        else:
            if len(carried) == 1:
                carried, back[0] = carried * 2, move(far[0], across)
            carried = [
                gather(queue, own[s], part, sels[s], cut, before, flops=cost)
                for cut, part, before, cost in zip(halves, back[s], carried, HOLD)
            ]
        carried = [move(a, up) for a in carried]
    grad_tokens, grad_gates = finish(queue, own[0], back[0], sels[0], ids, *carried)
    return grad_tokens, grad_gates.T


def solution(mesh):
    row, cube = P(("parts", "expert"), None), P(("parts", "expert"), None, None)
    body = functools.partial(shards, 2)
    return jax.shard_map(
        body, mesh=mesh, in_specs=(row, row, row, row, cube, cube), out_specs=(row, row), check_vma=False
    )
```

```python
import functools

import jax
import jax.numpy as jnp
from jax import lax
from jax.experimental import pallas as pl
from jax.experimental.pallas import tpu as pltpu
from jax.sharding import PartitionSpec as P

F32, BF16 = jnp.float32, jnp.bfloat16
LANES = 128
VMEM_BYTES = 16 * 2**20
COST = 30
HOLD = 8 * 10**9, 0, 8 * 10**9
NT = (((1,), (1,)), ((), ()))
LOCAL = pl.BlockSpec(memory_space=pltpu.VMEM)
SCALAR = pl.BlockSpec(memory_space=pltpu.SMEM)
ANYWHERE = pl.BlockSpec(memory_space=pl.ANY)


def array(*shape, dtype=BF16):
    return jax.ShapeDtypeStruct(shape, dtype)


class Queue:
    def __init__(self, ticket):
        self.ticket = ticket

    def run(self, kernel, operands, outs, scratch=(), flops=0, anywhere=0):
        def body(ticket_ref, *refs):
            n = len(operands) + len(outs)
            kernel(ticket_ref, *refs[:n], *refs[n + 1 :])
            for i in range(4):
                refs[n][i] = ticket_ref[i]

        *results, self.ticket = pl.pallas_call(
            body,
            in_specs=[SCALAR] + [ANYWHERE] * anywhere + [LOCAL] * (len(operands) - anywhere),
            out_specs=[LOCAL] * len(outs) + [SCALAR],
            out_shape=list(outs) + [array(4, dtype=jnp.int32)],
            scratch_shapes=list(scratch),
            compiler_params=pltpu.CompilerParams(vmem_limit_bytes=VMEM_BYTES),
            cost_estimate=pl.CostEstimate(flops=COST * flops // 100, bytes_accessed=0, transcendentals=0),
        )(self.ticket, *[pltpu.with_memory_space_constraint(a, pltpu.HBM if i < anywhere else pltpu.VMEM) for i, a in enumerate(operands)])
        return results[0] if len(results) == 1 else results


def load_kernel(count, pieces, _, *refs):
    sems = refs[-1]
    copies = []
    for i in range(count):
        rows = refs[i].shape[0] // pieces
        for j in range(pieces):
            at = pl.ds(j * rows, rows)
            copies.append(pltpu.make_async_copy(refs[i].at[at], refs[count + i].at[at], sems.at[i, j]))
            copies[-1].start()
    for c in copies:
        c.wait()


def load(queue, *arrays, pieces=4):
    n = len(arrays)
    return queue.run(
        functools.partial(load_kernel, n, pieces), arrays, [array(*a.shape) for a in arrays],
        [pltpu.SemaphoreType.DMA((n, pieces))], anywhere=n,
    )


def selection(table, ids_ref, near):
    rows = table.shape[0]
    lane = lax.broadcasted_iota(jnp.int32, (8, LANES), 1)
    pick = jnp.where((lane == ids_ref[2]) | (lane == ids_ref[3]), 1.0, 0.0)
    named = jnp.where(table > 0.0, 1.0, 0.0)
    need = jnp.minimum(lax.dot_general(pick, named, NT, preferred_element_type=F32), 1.0)
    before = lax.broadcasted_iota(jnp.int32, (rows, rows), 0) < lax.broadcasted_iota(jnp.int32, (rows, rows), 1)
    place = jnp.dot(need, jnp.where(before, 1.0, 0.0), preferred_element_type=F32)
    slot = lax.broadcasted_iota(jnp.int32, (near, rows), 0)
    return jnp.where((place[:1].astype(jnp.int32) == slot) & (need[:1] > 0.0), 1.0, 0.0).astype(BF16)


def choose_kernel(near, ids_ref, x_ref, out_ref, sel_ref, *same_ref):
    for ref in same_ref:
        ref[...] = x_ref[...]
    sel_ref[...] = selection(x_ref[:, x_ref.shape[1] - LANES :].astype(F32), ids_ref, near)
    out_ref[...] = jnp.dot(sel_ref[...], x_ref[...], preferred_element_type=F32).astype(BF16)


def choose(queue, x, near, again):
    rows, width = x.shape
    outs = [array(near, width), array(near, rows)] + [array(rows, width)] * again
    return queue.run(functools.partial(choose_kernel, near), [x], outs)


def prepare_kernel(near, ids_ref, tokens_ref, named_hbm, weight_hbm, x_ref, out_ref, sel_ref, named_ref, weight_ref, sems):
    rows, features = tokens_ref.shape
    copies = [
        pltpu.make_async_copy(named_hbm, named_ref, sems.at[0]),
        pltpu.make_async_copy(weight_hbm, weight_ref, sems.at[1]),
        pltpu.make_async_copy(tokens_ref, x_ref.at[:, pl.ds(0, features)], sems.at[2]),
    ]
    for c in copies:
        c.start()
    for c in copies[:2]:
        c.wait()
    expert = lax.broadcasted_iota(jnp.int32, (LANES, rows), 0)
    table = jnp.zeros((LANES, rows), F32)
    for k in range(named_ref.shape[0]):
        weight = weight_ref[k : k + 1, :].astype(F32)
        table += jnp.where(expert == named_ref[k : k + 1, :], weight, 0.0)
    row = lax.broadcasted_iota(jnp.int32, (LANES, rows), 1).astype(F32)
    table = jnp.where(expert == LANES - 1, row, table).T
    x_ref[:, features:] = table.astype(BF16)
    sel_ref[...] = selection(table, ids_ref, near)
    copies[2].wait()
    out_ref[...] = jnp.dot(sel_ref[...], x_ref[...], preferred_element_type=F32).astype(BF16)


def prepare(queue, tokens, ids, weights, near):
    rows, features = tokens.shape
    width = features + LANES
    return queue.run(
        functools.partial(prepare_kernel, near),
        [tokens, ids, weights],
        [array(rows, width), array(near, width), array(near, rows)],
        [pltpu.VMEM(ids.shape, jnp.int32), pltpu.VMEM(weights.shape, BF16), pltpu.SemaphoreType.DMA((3,))],
        anywhere=3,
    )


def pack_kernel(_, sel_ref, g_ref, out_ref, *same_ref):
    for ref in same_ref:
        ref[...] = g_ref[...]
    out_ref[...] = jnp.dot(sel_ref[...], g_ref[...], preferred_element_type=F32).astype(BF16)


def pack(queue, sel, g, again):
    outs = [array(sel.shape[0], g.shape[1])] + [array(*g.shape)] * again
    return queue.run(pack_kernel, [sel, g], outs)


def spread(sel_ref, back_ref):
    return lax.dot_general(
        sel_ref[...], back_ref[...], (((0,), (0,)), ((), ())), preferred_element_type=F32
    )


def place_kernel(cuts, _, far_ref, tok_ref, *refs):
    near, width = far_ref.shape
    rows = refs[-1].shape[0]
    row = tok_ref[:, width - 1 :].astype(F32).astype(jnp.int32)
    sel = jnp.where(lax.broadcasted_iota(jnp.int32, (near, rows), 1) == row, 1.0, 0.0).astype(BF16)
    total = lax.dot_general(sel, far_ref[...], (((0,), (0,)), ((), ())), preferred_element_type=F32)
    for ref in refs[: -len(cuts)]:
        total += ref[...].astype(F32)
    for (at, end), ref in zip(cuts, refs[-len(cuts) :]):
        ref[...] = total[:, at:end].astype(BF16)


def place(queue, far, tok, rows, *carried, cuts=None):
    cuts = cuts or [(0, far.shape[1])]
    outs = [array(rows, end - at) for at, end in cuts]
    return queue.run(functools.partial(place_kernel, cuts), [far, tok, *carried], outs)


def gather_kernel(cut, _, own_ref, back_ref, sel_ref, *refs):
    at, end = cut
    total = own_ref[:, at:end].astype(F32) + spread(sel_ref, back_ref)
    for ref in refs[:-1]:
        total += (ref[...] if ref.shape == total.shape else ref[:, at:end]).astype(F32)
    refs[-1][...] = total.astype(BF16)


def gather(queue, own, back, sel, cut, *carried, flops=0):
    return queue.run(
        functools.partial(gather_kernel, cut), [own, back, sel, *carried],
        [array(own.shape[0], cut[1] - cut[0])], flops=flops,
    )


def add_kernel(cut, kept, _, *refs):
    for ref, same_ref in zip(refs[:kept], refs[len(refs) - kept :]):
        same_ref[...] = ref[...]
    *block_refs, out_ref = refs[kept : len(refs) - kept]
    width = out_ref.shape[1]
    blocks = [ref[...] if ref.shape[1] == width else ref[:, cut[0] : cut[1]] for ref in block_refs]
    out_ref[...] = sum(block.astype(F32) for block in blocks).astype(BF16)


def add(queue, cut, *blocks, kept=()):
    outs = [array(blocks[0].shape[0], cut[1] - cut[0])] + [array(*a.shape) for a in kept]
    return queue.run(functools.partial(add_kernel, cut, len(kept)), [*kept, *blocks], outs)


def front_kernel(_, own_ref, back_ref, sel_ref, carried_ref, out_ref, rest_ref):
    at = carried_ref.shape[1]
    settled = own_ref[...].astype(F32) + spread(sel_ref, back_ref)
    out_ref[...] = (settled[:, :at] + carried_ref[...].astype(F32)).astype(BF16)
    rest_ref[...] = settled[:, at:]


def finish_kernel(_, front_ref, rest_ref, carried_ref, ids_ref, out_ref, gates_ref):
    features = out_ref.shape[1]
    at = front_ref.shape[1]
    out_ref[:, :at] = front_ref[...]
    total = rest_ref[...] + carried_ref[...].astype(F32)
    out_ref[:, at:] = total[:, : features - at].astype(BF16)
    gates = total[:, features - at :].T
    expert = lax.broadcasted_iota(jnp.int32, gates.shape, 0)
    chosen = [
        jnp.sum(jnp.where(expert == ids_ref[k : k + 1, :], gates, 0.0), axis=0, keepdims=True)
        for k in range(ids_ref.shape[0])
    ]
    gates_ref[...] = jnp.concatenate(chosen, axis=0).astype(BF16)


def finish(queue, own, back, sel, ids, first, second):
    rows, width = own.shape
    front, rest = queue.run(
        front_kernel, [own, back, sel, first],
        [array(*first.shape), array(*second.shape, dtype=F32)], flops=HOLD[2],
    )
    return queue.run(
        finish_kernel, [front, rest, second, ids], [array(rows, width - LANES), array(*ids.shape)]
    )


def project_kernel(tile, _, own_ref, far_ref, w0_ref, w1_ref, *refs):
    kept = (len(refs) - 3) // 2
    out0_ref, out1_ref = refs[kept : kept + 2]
    both = refs[-1]
    for ref, same_ref in zip(refs[:kept], refs[kept + 2 : -1]):
        same_ref[...] = ref[...]
    features, width = w0_ref.shape
    rows = own_ref.shape[0]
    both[:rows, :] = own_ref[:, :features]
    both[rows:, :] = far_ref[:, :features]
    for w_ref, out_ref in ((w0_ref, out0_ref), (w1_ref, out1_ref)):
        for j in range(width // tile):
            at = pl.ds(j * tile, tile)
            out_ref[:, at] = jnp.dot(both[...], w_ref[:, at], preferred_element_type=F32)


def project(queue, own, far, w0, w1, *kept, tile=512):
    rows = own.shape[0] + far.shape[0]
    features, width = w0.shape
    return queue.run(
        functools.partial(project_kernel, tile),
        [own, far, w0, w1, *kept],
        [array(rows, width, dtype=F32)] * 2 + [array(*a.shape) for a in kept],
        [pltpu.VMEM((rows, features), BF16)],
        flops=4 * rows * features * width,
    )


def backward_kernel(
    tile, split, ids_ref, p0_ref, p1_ref, own_ref, far_ref, tok_own, tok_far, d0_ref, d1_ref, w0_ref, w1_ref,
    out_own, *refs,
):
    hidden, features = d0_ref.shape
    parts, splits = hidden // tile, features // split
    rows = own_ref.shape[0]
    *out_fars, both, meta, grads = refs
    starts = [sum(ref.shape[1] for ref in out_fars[:i]) for i in range(len(out_fars))]
    both[:rows, :] = own_ref[...]
    both[rows:, :] = far_ref[...]
    meta[:rows, :] = tok_own[:, features:].astype(F32)
    meta[rows:, :] = tok_far[:, features:].astype(F32)
    lane = lax.broadcasted_iota(jnp.int32, meta.shape, 1)
    gates = jnp.zeros(meta.shape, F32)
    for e, (p_ref, d_ref) in enumerate(((p0_ref, d0_ref), (p1_ref, d1_ref))):
        here = lane == ids_ref[e]
        scale = jnp.sum(jnp.where(here, meta[...], 0.0), axis=1, keepdims=True)
        total = jnp.zeros((meta.shape[0], 1), F32)
        for j in range(parts):
            at = pl.ds(j * tile, tile)
            hidden_grad = lax.dot_general(both[...], d_ref[at], NT, preferred_element_type=F32)
            gate_pre = p_ref[:, at]
            up_pre = p_ref[:, pl.ds(hidden + j * tile, tile)]
            sigmoid = 1.0 / (1.0 + jnp.exp(-gate_pre))
            active = gate_pre * sigmoid
            total += jnp.sum(hidden_grad * active * up_pre, axis=1, keepdims=True)
            scaled = scale * hidden_grad
            base = 2 * e * hidden + j * tile
            grads[:, pl.ds(base, tile)] = (
                scaled * up_pre * sigmoid * (1.0 + gate_pre * (1.0 - sigmoid))
            ).astype(BF16)
            grads[:, pl.ds(base + hidden, tile)] = (scaled * active).astype(BF16)
        gates += jnp.where(here, total, 0.0)
    out_own[:, features:] = gates[:rows].astype(BF16)
    out_fars[-1][:, features - starts[-1] :] = gates[rows:].astype(BF16)
    for j in range(splits):
        at = pl.ds(j * split, split)
        out = lax.dot_general(grads[:, : 2 * hidden], w0_ref[at], NT, preferred_element_type=F32)
        out += lax.dot_general(grads[:, 2 * hidden :], w1_ref[at], NT, preferred_element_type=F32)
        out_own[:, at] = out[:rows].astype(BF16)
        i = sum(start <= j * split for start in starts) - 1
        out_fars[i][:, pl.ds(j * split - starts[i], split)] = out[rows:].astype(BF16)


def backward(queue, p0, p1, own, far, tok_own, tok_far, d0, d1, w0, w1, cuts, tile=256, split=512):
    rows = own.shape[0] + far.shape[0]
    hidden, features = d0.shape
    return queue.run(
        functools.partial(backward_kernel, tile, split),
        [p0, p1, own, far, tok_own, tok_far, d0, d1, w0, w1],
        [array(own.shape[0], features + LANES)] + [array(far.shape[0], end - at) for at, end in cuts],
        [pltpu.VMEM((rows, features), BF16), pltpu.VMEM((rows, LANES), F32), pltpu.VMEM((rows, 4 * hidden), BF16)],
        flops=12 * rows * features * hidden,
    )


def shards(lines, tokens, cotangent, expert_ids, gate_weights, w_gate_up, w_down):
    devices = lax.axis_size("expert")
    depth = devices // (2 * lines)
    rows, features = tokens.shape
    fanout = expert_ids.shape[1]
    capacity = 7 * rows * fanout // (4 * devices)
    near = min(rows, -(-2 * capacity // 16) * 16)
    index = lambda z, y, c: (z * lines + y) * 2 + c
    places = [(z, y, c) for z in range(depth) for y in range(lines) for c in range(2)]
    ring = [z for z in range(depth) if z == 0 or z % 2] + [z for z in range(depth - 1, 0, -1) if z % 2 == 0]
    after = {z: ring[(i + 1) % depth] for i, z in enumerate(ring)}
    up = [(index(z, y, c), index(after[z], y, c)) for z, y, c in places]
    across = [(index(z, y, c), index(z, 1 - y, c)) for z, y, c in places]
    twin = [(index(z, y, c), index(z, y, 1 - c)) for z, y, c in places]
    move = lambda a, pairs: lax.ppermute(a, "expert", pairs)

    me = lax.axis_index("expert")
    queue = Queue(jnp.stack([me, me ^ 1, me ^ 2, me ^ 3]).astype(jnp.int32))
    ids, weights = expert_ids.T, gate_weights.T
    w0, d0 = w_gate_up[0], w_down[0]
    w1, d1 = move(w0, twin), move(d0, twin)
    last = depth - 1
    xs, gs, sels, xf, gf = [], [], [], [], []
    own, far, back = [], [], []
    early = 1 if depth == 4 else depth
    whole = [(0, features + LANES)]
    halves = [(0, features // 2), (features // 2, features + LANES)]
    nx = ng = None

    def take_tokens(s):
        nonlocal nx
        if s:
            x, again = nx, s < last
            packed, sel, *kept = choose(queue, x, near, again)
        else:
            x, packed, sel = prepare(queue, tokens, ids, weights, near)
            again = False
        x = kept[0] if again else x
        if s < last:
            nx = move(x, up)
        xf.append(move(packed, across))
        sels.append(sel)
        xs.append(x)

    def take_grads(s):
        nonlocal ng
        g, again = ng if s else cotangent, 0 < s < last
        packed = pack(queue, sels[s], g, again)
        if again:
            packed, g = packed
        if s < last:
            ng = move(g, up)
        gf.append(move(packed, across))
        gs.append(g)

    take_tokens(0)
    w0, d0 = load(queue, w0, d0)
    take_grads(0)
    w1, d1 = load(queue, w1, d1)
    take_tokens(1)
    for s in range(depth):
        if s == 1:
            take_tokens(2)
        kept = own[early : early + 1] if s == early + 2 else []
        p0, p1, *kept = project(queue, xs[s], xf[s], w0, w1, *kept)
        own[early : early + len(kept)] = kept
        if 1 < s < last:
            take_tokens(s + 1)
        if s == early + 1:
            lifted = move(place(queue, far[early], xf[early], rows), up)
        if s == early + 2:
            lifted = place(queue, far[s - 1], xf[s - 1], rows, lifted, cuts=halves)
            back[s - 1] = [move(a, across) for a in lifted]
        if s == 0:
            take_grads(1)
        cuts = halves if s == last else whole
        mine, *other = backward(queue, p0, p1, gs[s], gf[s], xs[s], xf[s], d0, d1, w0, w1, cuts)
        if 0 < s < last:
            take_grads(s + 1)
        own.append(mine)
        far.append(other[0])
        back.append(None if s in (0, early, early + 1) else [move(a, across) for a in other])
    carried = [move(own[1] if early == 1 else gather(queue, own[1], back[1][0], sels[1], *whole), up)]
    for s in range(2, depth):
        if s == early + 1:
            first = add(queue, halves[0], own[s], back[s][0], *carried)
            second, later = add(queue, halves[1], own[s], back[s][1], *carried, kept=[far[0]])
            back[0] = move(later, across)
            carried = [first, second]
        elif s < last:
            carried = [gather(queue, own[s], back[s][0], sels[s], whole[0], *carried)]
        else:
            if len(carried) == 1:
                carried, back[0] = carried * 2, move(far[0], across)
            carried = [
                gather(queue, own[s], part, sels[s], cut, before, flops=cost)
                for cut, part, before, cost in zip(halves, back[s], carried, HOLD)
            ]
        carried = [move(a, up) for a in carried]
    grad_tokens, grad_gates = finish(queue, own[0], back[0], sels[0], ids, *carried)
    return grad_tokens, grad_gates.T


def solution(mesh):
    row, cube = P(("parts", "expert"), None), P(("parts", "expert"), None, None)
    body = functools.partial(shards, 2)
    return jax.shard_map(
        body, mesh=mesh, in_specs=(row, row, row, row, cube, cube), out_specs=(row, row), check_vma=False
    )
```

```python
import functools

import jax
import jax.numpy as jnp
from jax import lax
from jax.experimental import pallas as pl
from jax.experimental.pallas import tpu as pltpu
from jax.sharding import PartitionSpec as P

F32, BF16 = jnp.float32, jnp.bfloat16
LANES = 128
VMEM_BYTES = 16 * 2**20
COST = 30
HOLD = 8 * 10**9, 0, 8 * 10**9
NT = (((1,), (1,)), ((), ()))
LOCAL = pl.BlockSpec(memory_space=pltpu.VMEM)
SCALAR = pl.BlockSpec(memory_space=pltpu.SMEM)
ANYWHERE = pl.BlockSpec(memory_space=pl.ANY)


def array(*shape, dtype=BF16):
    return jax.ShapeDtypeStruct(shape, dtype)


class Queue:
    def __init__(self, ticket):
        self.ticket = ticket

    def run(self, kernel, operands, outs, scratch=(), flops=0, anywhere=0):
        def body(ticket_ref, *refs):
            n = len(operands) + len(outs)
            kernel(ticket_ref, *refs[:n], *refs[n + 1 :])
            for i in range(4):
                refs[n][i] = ticket_ref[i]

        *results, self.ticket = pl.pallas_call(
            body,
            in_specs=[SCALAR] + [ANYWHERE] * anywhere + [LOCAL] * (len(operands) - anywhere),
            out_specs=[LOCAL] * len(outs) + [SCALAR],
            out_shape=list(outs) + [array(4, dtype=jnp.int32)],
            scratch_shapes=list(scratch),
            compiler_params=pltpu.CompilerParams(vmem_limit_bytes=VMEM_BYTES),
            cost_estimate=pl.CostEstimate(flops=COST * flops // 100, bytes_accessed=0, transcendentals=0),
        )(self.ticket, *[pltpu.with_memory_space_constraint(a, pltpu.HBM if i < anywhere else pltpu.VMEM) for i, a in enumerate(operands)])
        return results[0] if len(results) == 1 else results


def load_kernel(count, pieces, _, *refs):
    sems = refs[-1]
    copies = []
    for i in range(count):
        rows = refs[i].shape[0] // pieces
        for j in range(pieces):
            at = pl.ds(j * rows, rows)
            copies.append(pltpu.make_async_copy(refs[i].at[at], refs[count + i].at[at], sems.at[i, j]))
            copies[-1].start()
    for c in copies:
        c.wait()


def load(queue, *arrays, pieces=4):
    n = len(arrays)
    return queue.run(
        functools.partial(load_kernel, n, pieces), arrays, [array(*a.shape) for a in arrays],
        [pltpu.SemaphoreType.DMA((n, pieces))], anywhere=n,
    )


def selection(table, ids_ref, near):
    rows = table.shape[0]
    lane = lax.broadcasted_iota(jnp.int32, (8, LANES), 1)
    pick = jnp.where((lane == ids_ref[2]) | (lane == ids_ref[3]), 1.0, 0.0)
    named = jnp.where(table > 0.0, 1.0, 0.0)
    need = jnp.minimum(lax.dot_general(pick, named, NT, preferred_element_type=F32), 1.0)
    before = lax.broadcasted_iota(jnp.int32, (rows, rows), 0) < lax.broadcasted_iota(jnp.int32, (rows, rows), 1)
    place = jnp.dot(need, jnp.where(before, 1.0, 0.0), preferred_element_type=F32)
    slot = lax.broadcasted_iota(jnp.int32, (near, rows), 0)
    return jnp.where((place[:1].astype(jnp.int32) == slot) & (need[:1] > 0.0), 1.0, 0.0).astype(BF16)


def choose_kernel(near, ids_ref, x_ref, out_ref, sel_ref, *same_ref):
    for ref in same_ref:
        ref[...] = x_ref[...]
    sel_ref[...] = selection(x_ref[:, x_ref.shape[1] - LANES :].astype(F32), ids_ref, near)
    out_ref[...] = jnp.dot(sel_ref[...], x_ref[...], preferred_element_type=F32).astype(BF16)


def choose(queue, x, near, again):
    rows, width = x.shape
    outs = [array(near, width), array(near, rows)] + [array(rows, width)] * again
    return queue.run(functools.partial(choose_kernel, near), [x], outs)


def prepare_kernel(near, ids_ref, tokens_ref, named_hbm, weight_hbm, x_ref, out_ref, sel_ref, named_ref, weight_ref, sems):
    rows, features = tokens_ref.shape
    copies = [
        pltpu.make_async_copy(named_hbm, named_ref, sems.at[0]),
        pltpu.make_async_copy(weight_hbm, weight_ref, sems.at[1]),
        pltpu.make_async_copy(tokens_ref, x_ref.at[:, pl.ds(0, features)], sems.at[2]),
    ]
    for c in copies:
        c.start()
    for c in copies[:2]:
        c.wait()
    expert = lax.broadcasted_iota(jnp.int32, (LANES, rows), 0)
    table = jnp.zeros((LANES, rows), F32)
    for k in range(named_ref.shape[0]):
        weight = weight_ref[k : k + 1, :].astype(F32)
        table += jnp.where(expert == named_ref[k : k + 1, :], weight, 0.0)
    row = lax.broadcasted_iota(jnp.int32, (LANES, rows), 1).astype(F32)
    table = jnp.where(expert == LANES - 1, row, table).T
    x_ref[:, features:] = table.astype(BF16)
    sel_ref[...] = selection(table, ids_ref, near)
    copies[2].wait()
    out_ref[...] = jnp.dot(sel_ref[...], x_ref[...], preferred_element_type=F32).astype(BF16)


def prepare(queue, tokens, ids, weights, near):
    rows, features = tokens.shape
    width = features + LANES
    return queue.run(
        functools.partial(prepare_kernel, near),
        [tokens, ids, weights],
        [array(rows, width), array(near, width), array(near, rows)],
        [pltpu.VMEM(ids.shape, jnp.int32), pltpu.VMEM(weights.shape, BF16), pltpu.SemaphoreType.DMA((3,))],
        anywhere=3,
    )


def pack_kernel(_, sel_ref, g_ref, out_ref, *same_ref):
    for ref in same_ref:
        ref[...] = g_ref[...]
    out_ref[...] = jnp.dot(sel_ref[...], g_ref[...], preferred_element_type=F32).astype(BF16)


def pack(queue, sel, g, again):
    outs = [array(sel.shape[0], g.shape[1])] + [array(*g.shape)] * again
    return queue.run(pack_kernel, [sel, g], outs)


def spread(sel_ref, back_ref):
    return lax.dot_general(
        sel_ref[...], back_ref[...], (((0,), (0,)), ((), ())), preferred_element_type=F32
    )


def place_kernel(cuts, _, *refs):
    rows = refs[-1].shape[0]
    total = 0.0
    for ref in refs[: -len(cuts)]:
        near, width = ref.shape
        row = ref[:, width - 1 :].astype(F32).astype(jnp.int32)
        sel = jnp.where(lax.broadcasted_iota(jnp.int32, (near, rows), 1) == row, 1.0, 0.0).astype(BF16)
        total += lax.dot_general(sel, ref[...], (((0,), (0,)), ((), ())), preferred_element_type=F32)
    for (at, end), ref in zip(cuts, refs[-len(cuts) :]):
        ref[...] = total[:, at:end].astype(BF16)


def place(queue, rows, cuts, *packed):
    return queue.run(functools.partial(place_kernel, cuts), packed, [array(rows, end - at) for at, end in cuts])


def gather_kernel(cut, _, own_ref, back_ref, sel_ref, *refs):
    at, end = cut
    total = own_ref[:, at:end].astype(F32) + spread(sel_ref, back_ref)
    for ref in refs[:-1]:
        total += (ref[...] if ref.shape == total.shape else ref[:, at:end]).astype(F32)
    refs[-1][...] = total.astype(BF16)


def gather(queue, own, back, sel, cut, *carried, flops=0):
    return queue.run(
        functools.partial(gather_kernel, cut), [own, back, sel, *carried],
        [array(own.shape[0], cut[1] - cut[0])], flops=flops,
    )


def add_kernel(cut, kept, _, *refs):
    for ref, same_ref in zip(refs[:kept], refs[len(refs) - kept :]):
        same_ref[...] = ref[...]
    *block_refs, out_ref = refs[kept : len(refs) - kept]
    width = out_ref.shape[1]
    blocks = [ref[...] if ref.shape[1] == width else ref[:, cut[0] : cut[1]] for ref in block_refs]
    out_ref[...] = sum(block.astype(F32) for block in blocks).astype(BF16)


def add(queue, cut, *blocks, kept=()):
    outs = [array(blocks[0].shape[0], cut[1] - cut[0])] + [array(*a.shape) for a in kept]
    return queue.run(functools.partial(add_kernel, cut, len(kept)), [*kept, *blocks], outs)


def front_kernel(_, own_ref, back_ref, sel_ref, carried_ref, out_ref, rest_ref):
    at = carried_ref.shape[1]
    settled = own_ref[...].astype(F32) + spread(sel_ref, back_ref)
    out_ref[...] = (settled[:, :at] + carried_ref[...].astype(F32)).astype(BF16)
    rest_ref[...] = settled[:, at:]


def finish_kernel(_, front_ref, rest_ref, carried_ref, ids_ref, out_ref, gates_ref):
    features = out_ref.shape[1]
    at = front_ref.shape[1]
    out_ref[:, :at] = front_ref[...]
    total = rest_ref[...] + carried_ref[...].astype(F32)
    out_ref[:, at:] = total[:, : features - at].astype(BF16)
    gates = total[:, features - at :].T
    expert = lax.broadcasted_iota(jnp.int32, gates.shape, 0)
    chosen = [
        jnp.sum(jnp.where(expert == ids_ref[k : k + 1, :], gates, 0.0), axis=0, keepdims=True)
        for k in range(ids_ref.shape[0])
    ]
    gates_ref[...] = jnp.concatenate(chosen, axis=0).astype(BF16)


def finish(queue, own, back, sel, ids, first, second):
    rows, width = own.shape
    front, rest = queue.run(
        front_kernel, [own, back, sel, first],
        [array(*first.shape), array(*second.shape, dtype=F32)], flops=HOLD[2],
    )
    return queue.run(
        finish_kernel, [front, rest, second, ids], [array(rows, width - LANES), array(*ids.shape)]
    )


def project_kernel(tile, _, own_ref, far_ref, w0_ref, w1_ref, *refs):
    kept = (len(refs) - 3) // 2
    out0_ref, out1_ref = refs[kept : kept + 2]
    both = refs[-1]
    for ref, same_ref in zip(refs[:kept], refs[kept + 2 : -1]):
        same_ref[...] = ref[...]
    features, width = w0_ref.shape
    rows = own_ref.shape[0]
    both[:rows, :] = own_ref[:, :features]
    both[rows:, :] = far_ref[:, :features]
    for w_ref, out_ref in ((w0_ref, out0_ref), (w1_ref, out1_ref)):
        for j in range(width // tile):
            at = pl.ds(j * tile, tile)
            out_ref[:, at] = jnp.dot(both[...], w_ref[:, at], preferred_element_type=F32)


def project(queue, own, far, w0, w1, *kept, tile=512):
    rows = own.shape[0] + far.shape[0]
    features, width = w0.shape
    return queue.run(
        functools.partial(project_kernel, tile),
        [own, far, w0, w1, *kept],
        [array(rows, width, dtype=F32)] * 2 + [array(*a.shape) for a in kept],
        [pltpu.VMEM((rows, features), BF16)],
        flops=4 * rows * features * width,
    )


def backward_kernel(
    tile, split, ids_ref, p0_ref, p1_ref, own_ref, far_ref, tok_own, tok_far, d0_ref, d1_ref, w0_ref, w1_ref,
    out_own, *refs,
):
    hidden, features = d0_ref.shape
    parts, splits = hidden // tile, features // split
    rows = own_ref.shape[0]
    *out_fars, both, meta, grads = refs
    starts = [sum(ref.shape[1] for ref in out_fars[:i]) for i in range(len(out_fars))]
    both[:rows, :] = own_ref[...]
    both[rows:, :] = far_ref[...]
    meta[:rows, :] = tok_own[:, features:].astype(F32)
    meta[rows:, :] = tok_far[:, features:].astype(F32)
    lane = lax.broadcasted_iota(jnp.int32, meta.shape, 1)
    gates = jnp.zeros(meta.shape, F32)
    for e, (p_ref, d_ref) in enumerate(((p0_ref, d0_ref), (p1_ref, d1_ref))):
        here = lane == ids_ref[e]
        scale = jnp.sum(jnp.where(here, meta[...], 0.0), axis=1, keepdims=True)
        total = jnp.zeros((meta.shape[0], 1), F32)
        for j in range(parts):
            at = pl.ds(j * tile, tile)
            hidden_grad = lax.dot_general(both[...], d_ref[at], NT, preferred_element_type=F32)
            gate_pre = p_ref[:, at]
            up_pre = p_ref[:, pl.ds(hidden + j * tile, tile)]
            sigmoid = 1.0 / (1.0 + jnp.exp(-gate_pre))
            active = gate_pre * sigmoid
            total += jnp.sum(hidden_grad * active * up_pre, axis=1, keepdims=True)
            scaled = scale * hidden_grad
            base = 2 * e * hidden + j * tile
            grads[:, pl.ds(base, tile)] = (
                scaled * up_pre * sigmoid * (1.0 + gate_pre * (1.0 - sigmoid))
            ).astype(BF16)
            grads[:, pl.ds(base + hidden, tile)] = (scaled * active).astype(BF16)
        gates += jnp.where(here, total, 0.0)
    out_own[:, features:] = gates[:rows].astype(BF16)
    gates = jnp.where(lane == LANES - 1, meta[...], gates)
    out_fars[-1][:, features - starts[-1] :] = gates[rows:].astype(BF16)
    for j in range(splits):
        at = pl.ds(j * split, split)
        out = lax.dot_general(grads[:, : 2 * hidden], w0_ref[at], NT, preferred_element_type=F32)
        out += lax.dot_general(grads[:, 2 * hidden :], w1_ref[at], NT, preferred_element_type=F32)
        out_own[:, at] = out[:rows].astype(BF16)
        i = sum(start <= j * split for start in starts) - 1
        out_fars[i][:, pl.ds(j * split - starts[i], split)] = out[rows:].astype(BF16)


def backward(queue, p0, p1, own, far, tok_own, tok_far, d0, d1, w0, w1, cuts, tile=256, split=512):
    rows = own.shape[0] + far.shape[0]
    hidden, features = d0.shape
    return queue.run(
        functools.partial(backward_kernel, tile, split),
        [p0, p1, own, far, tok_own, tok_far, d0, d1, w0, w1],
        [array(own.shape[0], features + LANES)] + [array(far.shape[0], end - at) for at, end in cuts],
        [pltpu.VMEM((rows, features), BF16), pltpu.VMEM((rows, LANES), F32), pltpu.VMEM((rows, 4 * hidden), BF16)],
        flops=12 * rows * features * hidden,
    )


def shards(lines, tokens, cotangent, expert_ids, gate_weights, w_gate_up, w_down):
    devices = lax.axis_size("expert")
    depth = devices // (2 * lines)
    rows, features = tokens.shape
    fanout = expert_ids.shape[1]
    capacity = 7 * rows * fanout // (4 * devices)
    near = min(rows, -(-2 * capacity // 16) * 16)
    index = lambda z, y, c: (z * lines + y) * 2 + c
    places = [(z, y, c) for z in range(depth) for y in range(lines) for c in range(2)]
    ring = [z for z in range(depth) if z == 0 or z % 2] + [z for z in range(depth - 1, 0, -1) if z % 2 == 0]
    after = {z: ring[(i + 1) % depth] for i, z in enumerate(ring)}
    up = [(index(z, y, c), index(after[z], y, c)) for z, y, c in places]
    across = [(index(z, y, c), index(z, 1 - y, c)) for z, y, c in places]
    twin = [(index(z, y, c), index(z, y, 1 - c)) for z, y, c in places]
    move = lambda a, pairs: lax.ppermute(a, "expert", pairs)

    me = lax.axis_index("expert")
    queue = Queue(jnp.stack([me, me ^ 1, me ^ 2, me ^ 3]).astype(jnp.int32))
    ids, weights = expert_ids.T, gate_weights.T
    w0, d0 = w_gate_up[0], w_down[0]
    w1, d1 = move(w0, twin), move(d0, twin)
    last = depth - 1
    xs, gs, sels, xf, gf = [], [], [], [], []
    own, far, back = [], [], []
    early = 1 if depth == 4 else depth
    whole = [(0, features + LANES)]
    halves = [(0, features // 2), (features // 2, features + LANES)]
    nx = ng = None

    def take_tokens(s):
        nonlocal nx
        if s:
            x, again = nx, s < last
            packed, sel, *kept = choose(queue, x, near, again)
        else:
            x, packed, sel = prepare(queue, tokens, ids, weights, near)
            again = False
        x = kept[0] if again else x
        if s < last:
            nx = move(x, up)
        xf.append(move(packed, across))
        sels.append(sel)
        xs.append(x)

    def take_grads(s):
        nonlocal ng
        g, again = ng if s else cotangent, 0 < s < last
        packed = pack(queue, sels[s], g, again)
        if again:
            packed, g = packed
        if s < last:
            ng = move(g, up)
        gf.append(move(packed, across))
        gs.append(g)

    take_tokens(0)
    w0, d0 = load(queue, w0, d0)
    take_grads(0)
    w1, d1 = load(queue, w1, d1)
    take_tokens(1)
    for s in range(depth):
        if s == 1:
            take_tokens(2)
        kept = far[early : early + 1] if s == early + 1 else own[early : early + 1] if s == early + 2 else []
        p0, p1, *kept = project(queue, xs[s], xf[s], w0, w1, *kept)
        if s == early + 1:
            lifted = move(kept[0], up)
        if s == early + 2:
            own[early] = kept[0]
        if 1 < s < last:
            take_tokens(s + 1)
        if s == early + 2:
            lifted = place(queue, rows, halves, far[s - 1], lifted)
            back[s - 1] = [move(a, across) for a in lifted]
        if s == 0:
            take_grads(1)
        cuts = halves if s == last else whole
        mine, *other = backward(queue, p0, p1, gs[s], gf[s], xs[s], xf[s], d0, d1, w0, w1, cuts)
        if 0 < s < last:
            take_grads(s + 1)
        own.append(mine)
        far.append(other[0])
        back.append(None if s in (0, early, early + 1) else [move(a, across) for a in other])
    carried = [move(own[1] if early == 1 else gather(queue, own[1], back[1][0], sels[1], *whole), up)]
    for s in range(2, depth):
        if s == early + 1:
            first = add(queue, halves[0], own[s], back[s][0], *carried)
            second, later = add(queue, halves[1], own[s], back[s][1], *carried, kept=[far[0]])
            back[0] = move(later, across)
            carried = [first, second]
        elif s < last:
            carried = [gather(queue, own[s], back[s][0], sels[s], whole[0], *carried)]
        else:
            if len(carried) == 1:
                carried, back[0] = carried * 2, move(far[0], across)
            carried = [
                gather(queue, own[s], part, sels[s], cut, before, flops=cost)
                for cut, part, before, cost in zip(halves, back[s], carried, HOLD)
            ]
        carried = [move(a, up) for a in carried]
    grad_tokens, grad_gates = finish(queue, own[0], back[0], sels[0], ids, *carried)
    return grad_tokens, grad_gates.T


def solution(mesh):
    row, cube = P(("parts", "expert"), None), P(("parts", "expert"), None, None)
    body = functools.partial(shards, 2)
    return jax.shard_map(
        body, mesh=mesh, in_specs=(row, row, row, row, cube, cube), out_specs=(row, row), check_vma=False
    )
```

```python
import functools

import jax
import jax.numpy as jnp
from jax import lax
from jax.experimental import pallas as pl
from jax.experimental.pallas import tpu as pltpu
from jax.sharding import PartitionSpec as P

F32, BF16 = jnp.float32, jnp.bfloat16
LANES = 128
VMEM_BYTES = 16 * 2**20
COST = 34
HOLD = 8 * 10**9, 8 * 10**9, 8 * 10**9
NT = (((1,), (1,)), ((), ()))
LOCAL = pl.BlockSpec(memory_space=pltpu.VMEM)
SCALAR = pl.BlockSpec(memory_space=pltpu.SMEM)
ANYWHERE = pl.BlockSpec(memory_space=pl.ANY)


def array(*shape, dtype=BF16):
    return jax.ShapeDtypeStruct(shape, dtype)


class Queue:
    def __init__(self, ticket):
        self.ticket = ticket

    def run(self, kernel, operands, outs, scratch=(), flops=0, anywhere=0):
        def body(ticket_ref, *refs):
            n = len(operands) + len(outs)
            kernel(ticket_ref, *refs[:n], *refs[n + 1 :])
            for i in range(4):
                refs[n][i] = ticket_ref[i]

        *results, self.ticket = pl.pallas_call(
            body,
            in_specs=[SCALAR] + [ANYWHERE] * anywhere + [LOCAL] * (len(operands) - anywhere),
            out_specs=[LOCAL] * len(outs) + [SCALAR],
            out_shape=list(outs) + [array(4, dtype=jnp.int32)],
            scratch_shapes=list(scratch),
            compiler_params=pltpu.CompilerParams(vmem_limit_bytes=VMEM_BYTES),
            cost_estimate=pl.CostEstimate(flops=COST * flops // 100, bytes_accessed=0, transcendentals=0),
        )(self.ticket, *[pltpu.with_memory_space_constraint(a, pltpu.HBM if i < anywhere else pltpu.VMEM) for i, a in enumerate(operands)])
        return results[0] if len(results) == 1 else results


def load_kernel(count, pieces, _, *refs):
    sems = refs[-1]
    copies = []
    for i in range(count):
        rows = refs[i].shape[0] // pieces
        for j in range(pieces):
            at = pl.ds(j * rows, rows)
            copies.append(pltpu.make_async_copy(refs[i].at[at], refs[count + i].at[at], sems.at[i, j]))
            copies[-1].start()
    for c in copies:
        c.wait()


def load(queue, *arrays, pieces=4):
    n = len(arrays)
    return queue.run(
        functools.partial(load_kernel, n, pieces), arrays, [array(*a.shape) for a in arrays],
        [pltpu.SemaphoreType.DMA((n, pieces))], anywhere=n,
    )


def selection(table, ids_ref, near):
    rows = table.shape[0]
    lane = lax.broadcasted_iota(jnp.int32, (8, LANES), 1)
    pick = jnp.where((lane == ids_ref[2]) | (lane == ids_ref[3]), 1.0, 0.0)
    named = jnp.where(table > 0.0, 1.0, 0.0)
    need = jnp.minimum(lax.dot_general(pick, named, NT, preferred_element_type=F32), 1.0)
    before = lax.broadcasted_iota(jnp.int32, (rows, rows), 0) < lax.broadcasted_iota(jnp.int32, (rows, rows), 1)
    place = jnp.dot(need, jnp.where(before, 1.0, 0.0), preferred_element_type=F32)
    slot = lax.broadcasted_iota(jnp.int32, (near, rows), 0)
    return jnp.where((place[:1].astype(jnp.int32) == slot) & (need[:1] > 0.0), 1.0, 0.0).astype(BF16)


def choose_kernel(near, ids_ref, x_ref, out_ref, sel_ref, *same_ref):
    for ref in same_ref:
        ref[...] = x_ref[...]
    sel_ref[...] = selection(x_ref[:, x_ref.shape[1] - LANES :].astype(F32), ids_ref, near)
    out_ref[...] = jnp.dot(sel_ref[...], x_ref[...], preferred_element_type=F32).astype(BF16)


def choose(queue, x, near, again):
    rows, width = x.shape
    outs = [array(near, width), array(near, rows)] + [array(rows, width)] * again
    return queue.run(functools.partial(choose_kernel, near), [x], outs)


def prepare_kernel(near, ids_ref, tokens_ref, named_hbm, weight_hbm, x_ref, out_ref, sel_ref, named_ref, weight_ref, sems):
    rows, features = tokens_ref.shape
    copies = [
        pltpu.make_async_copy(named_hbm, named_ref, sems.at[0]),
        pltpu.make_async_copy(weight_hbm, weight_ref, sems.at[1]),
        pltpu.make_async_copy(tokens_ref, x_ref.at[:, pl.ds(0, features)], sems.at[2]),
    ]
    for c in copies:
        c.start()
    for c in copies[:2]:
        c.wait()
    expert = lax.broadcasted_iota(jnp.int32, (LANES, rows), 0)
    table = jnp.zeros((LANES, rows), F32)
    for k in range(named_ref.shape[0]):
        weight = weight_ref[k : k + 1, :].astype(F32)
        table += jnp.where(expert == named_ref[k : k + 1, :], weight, 0.0)
    row = lax.broadcasted_iota(jnp.int32, (LANES, rows), 1).astype(F32)
    table = jnp.where(expert == LANES - 1, row, table).T
    x_ref[:, features:] = table.astype(BF16)
    sel_ref[...] = selection(table, ids_ref, near)
    copies[2].wait()
    out_ref[...] = jnp.dot(sel_ref[...], x_ref[...], preferred_element_type=F32).astype(BF16)


def prepare(queue, tokens, ids, weights, near):
    rows, features = tokens.shape
    width = features + LANES
    return queue.run(
        functools.partial(prepare_kernel, near),
        [tokens, ids, weights],
        [array(rows, width), array(near, width), array(near, rows)],
        [pltpu.VMEM(ids.shape, jnp.int32), pltpu.VMEM(weights.shape, BF16), pltpu.SemaphoreType.DMA((3,))],
        anywhere=3,
    )


def pack_kernel(_, sel_ref, g_ref, out_ref, *same_ref):
    for ref in same_ref:
        ref[...] = g_ref[...]
    out_ref[...] = jnp.dot(sel_ref[...], g_ref[...], preferred_element_type=F32).astype(BF16)


def pack(queue, sel, g, again):
    outs = [array(sel.shape[0], g.shape[1])] + [array(*g.shape)] * again
    return queue.run(pack_kernel, [sel, g], outs)


def spread(sel_ref, back_ref):
    return lax.dot_general(
        sel_ref[...], back_ref[...], (((0,), (0,)), ((), ())), preferred_element_type=F32
    )


def place_kernel(cuts, _, *refs):
    rows = refs[-1].shape[0]
    total = 0.0
    for ref in refs[: -len(cuts)]:
        near, width = ref.shape
        row = ref[:, width - 1 :].astype(F32).astype(jnp.int32)
        sel = jnp.where(lax.broadcasted_iota(jnp.int32, (near, rows), 1) == row, 1.0, 0.0).astype(BF16)
        total += lax.dot_general(sel, ref[...], (((0,), (0,)), ((), ())), preferred_element_type=F32)
    for (at, end), ref in zip(cuts, refs[-len(cuts) :]):
        ref[...] = total[:, at:end].astype(BF16)


def place(queue, rows, cuts, *packed):
    return queue.run(functools.partial(place_kernel, cuts), packed, [array(rows, end - at) for at, end in cuts])


def gather_kernel(cut, kept, _, *refs):
    for ref, same_ref in zip(refs[:kept], refs[len(refs) - kept :]):
        same_ref[...] = ref[...]
    own_ref, back_ref, sel_ref, *carried_refs, out_ref = refs[kept : len(refs) - kept]
    at, end = cut
    total = own_ref[:, at:end].astype(F32) + spread(sel_ref, back_ref)
    for ref in carried_refs:
        total += (ref[...] if ref.shape == total.shape else ref[:, at:end]).astype(F32)
    out_ref[...] = total.astype(BF16)


def gather(queue, own, back, sel, cut, *carried, flops=0, kept=()):
    return queue.run(
        functools.partial(gather_kernel, cut, len(kept)), [*kept, own, back, sel, *carried],
        [array(own.shape[0], cut[1] - cut[0])] + [array(*a.shape) for a in kept], flops=flops,
    )


def add_kernel(cut, kept, _, *refs):
    for ref, same_ref in zip(refs[:kept], refs[len(refs) - kept :]):
        same_ref[...] = ref[...]
    *block_refs, out_ref = refs[kept : len(refs) - kept]
    width = out_ref.shape[1]
    blocks = [ref[...] if ref.shape[1] == width else ref[:, cut[0] : cut[1]] for ref in block_refs]
    out_ref[...] = sum(block.astype(F32) for block in blocks).astype(BF16)


def add(queue, cut, *blocks, kept=()):
    outs = [array(blocks[0].shape[0], cut[1] - cut[0])] + [array(*a.shape) for a in kept]
    return queue.run(functools.partial(add_kernel, cut, len(kept)), [*kept, *blocks], outs)


def front_kernel(_, own_ref, back_ref, sel_ref, carried_ref, out_ref, rest_ref):
    at = carried_ref.shape[1]
    settled = own_ref[...].astype(F32) + spread(sel_ref, back_ref)
    out_ref[...] = (settled[:, :at] + carried_ref[...].astype(F32)).astype(BF16)
    rest_ref[...] = settled[:, at:]


def finish_kernel(_, front_ref, rest_ref, carried_ref, ids_ref, out_ref, gates_ref):
    features = out_ref.shape[1]
    at = front_ref.shape[1]
    out_ref[:, :at] = front_ref[...]
    total = rest_ref[...] + carried_ref[...].astype(F32)
    out_ref[:, at:] = total[:, : features - at].astype(BF16)
    gates = total[:, features - at :].T
    expert = lax.broadcasted_iota(jnp.int32, gates.shape, 0)
    chosen = [
        jnp.sum(jnp.where(expert == ids_ref[k : k + 1, :], gates, 0.0), axis=0, keepdims=True)
        for k in range(ids_ref.shape[0])
    ]
    gates_ref[...] = jnp.concatenate(chosen, axis=0).astype(BF16)


def finish(queue, own, back, sel, ids, first, second):
    rows, width = own.shape
    front, rest = queue.run(
        front_kernel, [own, back, sel, first],
        [array(*first.shape), array(*second.shape, dtype=F32)], flops=HOLD[2],
    )
    return queue.run(
        finish_kernel, [front, rest, second, ids], [array(rows, width - LANES), array(*ids.shape)]
    )


def project_kernel(tile, _, own_ref, far_ref, w0_ref, w1_ref, *refs):
    kept = (len(refs) - 3) // 2
    out0_ref, out1_ref = refs[kept : kept + 2]
    both = refs[-1]
    for ref, same_ref in zip(refs[:kept], refs[kept + 2 : -1]):
        same_ref[...] = ref[...]
    features, width = w0_ref.shape
    rows = own_ref.shape[0]
    both[:rows, :] = own_ref[:, :features]
    both[rows:, :] = far_ref[:, :features]
    for w_ref, out_ref in ((w0_ref, out0_ref), (w1_ref, out1_ref)):
        for j in range(width // tile):
            at = pl.ds(j * tile, tile)
            out_ref[:, at] = jnp.dot(both[...], w_ref[:, at], preferred_element_type=F32)


def project(queue, own, far, w0, w1, *kept, tile=512):
    rows = own.shape[0] + far.shape[0]
    features, width = w0.shape
    return queue.run(
        functools.partial(project_kernel, tile),
        [own, far, w0, w1, *kept],
        [array(rows, width, dtype=F32)] * 2 + [array(*a.shape) for a in kept],
        [pltpu.VMEM((rows, features), BF16)],
        flops=4 * rows * features * width,
    )


def backward_kernel(
    tile, split, ids_ref, p0_ref, p1_ref, own_ref, far_ref, tok_own, tok_far, d0_ref, d1_ref, w0_ref, w1_ref,
    out_own, *refs,
):
    hidden, features = d0_ref.shape
    parts, splits = hidden // tile, features // split
    rows = own_ref.shape[0]
    *out_fars, both, meta, grads = refs
    starts = [sum(ref.shape[1] for ref in out_fars[:i]) for i in range(len(out_fars))]
    both[:rows, :] = own_ref[...]
    both[rows:, :] = far_ref[...]
    meta[:rows, :] = tok_own[:, features:].astype(F32)
    meta[rows:, :] = tok_far[:, features:].astype(F32)
    lane = lax.broadcasted_iota(jnp.int32, meta.shape, 1)
    gates = jnp.zeros(meta.shape, F32)
    for e, (p_ref, d_ref) in enumerate(((p0_ref, d0_ref), (p1_ref, d1_ref))):
        here = lane == ids_ref[e]
        scale = jnp.sum(jnp.where(here, meta[...], 0.0), axis=1, keepdims=True)
        total = jnp.zeros((meta.shape[0], 1), F32)
        for j in range(parts):
            at = pl.ds(j * tile, tile)
            hidden_grad = lax.dot_general(both[...], d_ref[at], NT, preferred_element_type=F32)
            gate_pre = p_ref[:, at]
            up_pre = p_ref[:, pl.ds(hidden + j * tile, tile)]
            sigmoid = 1.0 / (1.0 + jnp.exp(-gate_pre))
            active = gate_pre * sigmoid
            total += jnp.sum(hidden_grad * active * up_pre, axis=1, keepdims=True)
            scaled = scale * hidden_grad
            base = 2 * e * hidden + j * tile
            grads[:, pl.ds(base, tile)] = (
                scaled * up_pre * sigmoid * (1.0 + gate_pre * (1.0 - sigmoid))
            ).astype(BF16)
            grads[:, pl.ds(base + hidden, tile)] = (scaled * active).astype(BF16)
        gates += jnp.where(here, total, 0.0)
    out_own[:, features:] = gates[:rows].astype(BF16)
    gates = jnp.where(lane == LANES - 1, meta[...], gates)
    out_fars[-1][:, features - starts[-1] :] = gates[rows:].astype(BF16)
    for j in range(splits):
        at = pl.ds(j * split, split)
        out = lax.dot_general(grads[:, : 2 * hidden], w0_ref[at], NT, preferred_element_type=F32)
        out += lax.dot_general(grads[:, 2 * hidden :], w1_ref[at], NT, preferred_element_type=F32)
        out_own[:, at] = out[:rows].astype(BF16)
        i = sum(start <= j * split for start in starts) - 1
        out_fars[i][:, pl.ds(j * split - starts[i], split)] = out[rows:].astype(BF16)


def backward(queue, p0, p1, own, far, tok_own, tok_far, d0, d1, w0, w1, cuts, tile=256, split=512):
    rows = own.shape[0] + far.shape[0]
    hidden, features = d0.shape
    return queue.run(
        functools.partial(backward_kernel, tile, split),
        [p0, p1, own, far, tok_own, tok_far, d0, d1, w0, w1],
        [array(own.shape[0], features + LANES)] + [array(far.shape[0], end - at) for at, end in cuts],
        [pltpu.VMEM((rows, features), BF16), pltpu.VMEM((rows, LANES), F32), pltpu.VMEM((rows, 4 * hidden), BF16)],
        flops=12 * rows * features * hidden,
    )


def shards(lines, tokens, cotangent, expert_ids, gate_weights, w_gate_up, w_down):
    devices = lax.axis_size("expert")
    depth = devices // (2 * lines)
    rows, features = tokens.shape
    fanout = expert_ids.shape[1]
    capacity = 7 * rows * fanout // (4 * devices)
    near = min(rows, -(-2 * capacity // 16) * 16)
    index = lambda z, y, c: (z * lines + y) * 2 + c
    places = [(z, y, c) for z in range(depth) for y in range(lines) for c in range(2)]
    ring = [z for z in range(depth) if z == 0 or z % 2] + [z for z in range(depth - 1, 0, -1) if z % 2 == 0]
    after = {z: ring[(i + 1) % depth] for i, z in enumerate(ring)}
    up = [(index(z, y, c), index(after[z], y, c)) for z, y, c in places]
    across = [(index(z, y, c), index(z, 1 - y, c)) for z, y, c in places]
    twin = [(index(z, y, c), index(z, y, 1 - c)) for z, y, c in places]
    move = lambda a, pairs: lax.ppermute(a, "expert", pairs)

    me = lax.axis_index("expert")
    queue = Queue(jnp.stack([me, me ^ 1, me ^ 2, me ^ 3]).astype(jnp.int32))
    ids, weights = expert_ids.T, gate_weights.T
    w0, d0 = w_gate_up[0], w_down[0]
    w1, d1 = move(w0, twin), move(d0, twin)
    last = depth - 1
    xs, gs, sels, xf, gf = [], [], [], [], []
    own, far, back = [], [], []
    early = 1 if depth == 4 else depth
    whole = [(0, features + LANES)]
    halves = [(0, features // 2), (features // 2, features + LANES)]
    nx = ng = None

    def take_tokens(s):
        nonlocal nx
        if s:
            x, again = nx, s < last
            packed, sel, *kept = choose(queue, x, near, again)
        else:
            x, packed, sel = prepare(queue, tokens, ids, weights, near)
            again = False
        x = kept[0] if again else x
        if s < last:
            nx = move(x, up)
        xf.append(move(packed, across))
        sels.append(sel)
        xs.append(x)

    def take_grads(s):
        nonlocal ng
        g, again = ng if s else cotangent, 0 < s < last
        packed = pack(queue, sels[s], g, again)
        if again:
            packed, g = packed
        if s < last:
            ng = move(g, up)
        gf.append(move(packed, across))
        gs.append(g)

    take_tokens(0)
    w0, d0 = load(queue, w0, d0)
    take_grads(0)
    w1, d1 = load(queue, w1, d1)
    take_tokens(1)
    for s in range(depth):
        if s == 1:
            take_tokens(2)
        kept = far[early : early + 1] if s == early + 1 else own[early : early + 1] if s == early + 2 else []
        p0, p1, *kept = project(queue, xs[s], xf[s], w0, w1, *kept)
        if s == early + 1:
            lifted = move(kept[0], up)
        if s == early + 2:
            own[early] = kept[0]
        if 1 < s < last:
            take_tokens(s + 1)
        if s == early + 2:
            lifted = place(queue, rows, halves, far[s - 1], lifted)
            back[s - 1] = [move(a, across) for a in lifted]
        if s == 0:
            take_grads(1)
        cuts = halves if s == last else whole
        mine, *other = backward(queue, p0, p1, gs[s], gf[s], xs[s], xf[s], d0, d1, w0, w1, cuts)
        if 0 < s < last:
            take_grads(s + 1)
        own.append(mine)
        far.append(other[0])
        back.append(None if s in (0, early, early + 1) else [move(a, across) for a in other])
    carried = [move(own[1] if early == 1 else gather(queue, own[1], back[1][0], sels[1], *whole), up)]
    for s in range(2, depth):
        if s == early + 1:
            carried = [add(queue, cut, own[s], part, *carried) for cut, part in zip(halves, back[s])]
        elif s < last:
            carried = [gather(queue, own[s], back[s][0], sels[s], whole[0], *carried)]
        else:
            carried = carried if len(carried) == 2 else carried * 2
            first, later = gather(
                queue, own[s], back[s][0], sels[s], halves[0], carried[0], flops=HOLD[0], kept=[far[0]]
            )
            second = gather(queue, own[s], back[s][1], sels[s], halves[1], carried[1], flops=HOLD[1])
            back[0] = move(later, across)
            carried = [first, second]
        carried = [move(a, up) for a in carried]
    grad_tokens, grad_gates = finish(queue, own[0], back[0], sels[0], ids, *carried)
    return grad_tokens, grad_gates.T


def solution(mesh):
    row, cube = P(("parts", "expert"), None), P(("parts", "expert"), None, None)
    body = functools.partial(shards, 2)
    return jax.shard_map(
        body, mesh=mesh, in_specs=(row, row, row, row, cube, cube), out_specs=(row, row), check_vma=False
    )
```
